256 devices in a mesh: ctx: 16 (over z, x_lo), head: 8 (over x_hi, y), dp: 2 (over core).
Axes of the slice: x: 4 (x_hi: 2, x_lo: 2; x = x_hi * 2 + x_lo), y: 4, z: 8, core: 2. Of those that a mesh axis runs over, the one named last changes fastest.
Arguments:
- queries: bfloat16 [2, 2048, 8192], P('dp', 'ctx', 'head'), may hold values from -16 to 16
- keys: bfloat16 [2, 2048, 1024], P('dp', 'ctx', 'head'), may hold values from -16 to 16
- values: bfloat16 [2, 2048, 1024], P('dp', 'ctx', 'head'), may hold values from -6 to 6
- grad_out: bfloat16 [2, 2048, 8192], P('dp', 'ctx', 'head'), may hold values from -6 to 6
- layer_inputs: bfloat16 [2, 2048, 5120], P('dp', ('ctx', 'head')), may hold values from -24 to 24
- doc_ids: int32 [2, 2048], P('dp'), may hold values from 0 to 7, never falling along the last dimension, each value on 1 to 512 neighbouring positions
- member_rank: int32 [16], replicated, may hold values from -1 to 14, as said below
- take_count: int32 [16], replicated, may hold values from 0 to 32, as said below
Outputs:
- grad_q: bfloat16 [2, 2048, 8192], P('dp', 'ctx', 'head')
- grad_k: bfloat16 [2, 2048, 1024], P('dp', 'ctx', 'head')
- grad_v: bfloat16 [2, 2048, 1024], P('dp', 'ctx', 'head')
- grad_wkv: float32 [5120, 2, 1024], P(('ctx', 'dp'), None, 'head')
The draws below stay inside these ranges and needn't reach their ends.
Inputs may be any that keep to these rules, and one draw needn't show every extreme that they name: `member_rank`: exactly one block holds -1; the others hold 0 to 14 in block order, skipping it. `take_count`: 0 for the excluded block; the counts sum to 128, and one member takes exactly 32.
All inputs are finite; a program needn't handle non-finite values.
Results may differ from the reference program's by a relative error of at most 0.0052.
Values may be sent and summed in bfloat16 or wider, within the bound.
A program may use at most 64 MiB of HBM per device.

```python
import math
import jax
import jax.numpy as jnp
import numpy as np
from jax import lax

D = 5120
H = 64
KVH = 8
HD = 128
TOK_DEV = 128
BATCH = 2
SEQ = 2048
N_CTX = 16


def member_plan(key):
    member_indices = jnp.arange(N_CTX, dtype=jnp.int32)
    excluded = jax.random.randint(jax.random.fold_in(key, 137), (), 0, N_CTX, dtype=jnp.int32)
    picked = jax.random.randint(jax.random.fold_in(key, 139), (), 0, N_CTX - 1, dtype=jnp.int32)
    heaviest_member = picked + (picked >= excluded).astype(jnp.int32)
    remaining_members = (member_indices != excluded) & (member_indices != heaviest_member)
    weights = jax.random.randint(jax.random.fold_in(key, 149), (N_CTX,), 1, 3, dtype=jnp.int32) * remaining_members.astype(jnp.int32)
    largest_row_count = TOK_DEV // 4
    remain = TOK_DEV - largest_row_count
    baseline_row_count = remain * weights // jnp.sum(weights)
    remainder_rows = remain - jnp.sum(baseline_row_count)
    rank_indices = jnp.cumsum(remaining_members.astype(jnp.int32)) - 1
    extra_share = (remaining_members & (rank_indices < remainder_rows)).astype(jnp.int32)
    member_counts = baseline_row_count + extra_share + jnp.where(member_indices == heaviest_member, largest_row_count, 0)
    ranks = member_indices - (member_indices > excluded).astype(jnp.int32)
    ranks = jnp.where(member_indices == excluded, -1, ranks)
    return (ranks.astype(jnp.int32), member_counts.astype(jnp.int32))


def row_scales(key, shape):
    return jnp.exp(jax.random.uniform(key, shape, minval=math.log(0.3), maxval=math.log(3.0)))


def draw_member_rank(key, part):
    ranks, member_counts = member_plan(key)
    return ranks


def draw_take_count(key, part):
    ranks, member_counts = member_plan(key)
    return member_counts


def draw_queries(key, part):
    key = jax.random.fold_in(key, 3)
    factor = row_scales(jax.random.fold_in(key, 1), (BATCH, SEQ, 1))
    base = jnp.clip(jax.random.normal(jax.random.fold_in(key, 2), (BATCH, SEQ, H * HD)), -5.0, 5.0) * factor
    return base.astype(jnp.bfloat16)


def draw_keys(key, part):
    key = jax.random.fold_in(key, 4)
    factor = row_scales(jax.random.fold_in(key, 1), (BATCH, SEQ, 1))
    base = jnp.clip(jax.random.normal(jax.random.fold_in(key, 2), (BATCH, SEQ, KVH * HD)), -5.0, 5.0) * factor
    return base.astype(jnp.bfloat16)


def spiked(drawn, stream_key, source, target, blocks, factor):
    def block_of(dim):
        return (jnp.arange(drawn.shape[dim]) // (drawn.shape[dim] // blocks)).reshape((-1,) + (1,) * (drawn.ndim - 1 - dim))

    one_side = jax.random.permutation(stream_key, blocks)[block_of(target)]
    other_side = (block_of(target) + blocks // 2) % blocks
    return jnp.where((block_of(source) == one_side) | (block_of(source) == other_side), factor * drawn, drawn)


def block_levels(rng, dims, split, least, high):
    loudness = 1.0
    for dim, blocks in split:
        steps = jax.random.uniform(jax.random.fold_in(jax.random.fold_in(rng, 6), dim), (blocks,), jnp.float32, least / len(split), high / len(split))
        loudness = loudness * jnp.repeat(jnp.exp(steps), dims[dim] // blocks).reshape((-1,) + (1,) * (len(dims) - 1 - dim))
    return loudness


def length_profile(amount, total, most, slope):
    portions = [(1 << 20) // math.isqrt(grade ** slope) + 1 for grade in range(2, amount + 1)]
    rest, counts = total - most - (amount - 1), [1] * (amount - 1)
    while rest > 0:
        free = [i for i in range(amount - 1) if counts[i] < most]
        whole, left = sum([portions[i] for i in free]), rest
        for i in free:
            addition = min(most - counts[i], max(1, left * portions[i] // whole), rest)
            counts[i] = counts[i] + addition
            rest = rest - addition
    return np.array([most] + counts)


def ragged(stream_key, count, total, most, lean):
    if count == 2:
        one = jax.random.randint(stream_key, (), max(1, total - most), min(most, total - 1) + 1)
        return jnp.stack([one, total - one])
    tallies = jnp.asarray(length_profile(count, total, most, lean), jnp.int32)
    pairs = (count - 1) // 2
    giver, taker = tallies[1:1 + 2 * pairs:2], tallies[2:2 + 2 * pairs:2]
    margin = jnp.minimum(giver - 1, most - taker)
    moved = jax.random.randint(jax.random.fold_in(stream_key, 1), (pairs,), 0, 1 << 20) % (margin + 1)
    tallies = tallies.at[1:1 + 2 * pairs:2].set(giver - moved).at[2:2 + 2 * pairs:2].set(taker + moved)
    return tallies[jax.random.permutation(jax.random.fold_in(stream_key, 2), count)]


def gaussian(own_key, extent, width, most, pieces=(), held_as=jnp.bfloat16):
    gain = block_levels(own_key, extent, pieces, -0.22, 0.18) if pieces else 1.0
    array = jax.random.normal(own_key, extent, jnp.float32) * width * gain
    return jnp.minimum(jnp.maximum(array, -most), most).astype(held_as)


def bell_draw_with(key, dims, spread, bound, pieces, heavy, held_as=jnp.bfloat16):
    drawn = spread * jax.random.normal(key, dims, jnp.float32)
    if pieces:
        drawn = drawn * block_levels(key, dims, pieces, -0.22, 0.18)
    return jnp.clip(spiked(drawn, jax.random.fold_in(key, 3), *heavy), -bound, bound).astype(held_as)


def setup_inputs(seed: int = 0) -> dict:
    splits = jax.random.split(jax.random.key(seed), 9)
    return {
        "queries": draw_queries(jax.random.fold_in(splits[8], 71), 0),
        "keys": draw_keys(jax.random.fold_in(splits[8], 71), 0),
        "values": gaussian(splits[2], (BATCH, SEQ, KVH * HD), 1.0, 6.0, ((0, 2), (1, 16), (2, 8))),
        "grad_out": gaussian(splits[3], (BATCH, SEQ, H * HD), 1.0, 6.0, ((0, 2), (1, 16), (2, 8))),
        "layer_inputs": bell_draw_with(splits[4], (BATCH, SEQ, D), 1.0, 24.0, ((0, 2), (1, 128)), (1, 2, 128, 5.5)),
        "doc_ids": jax.vmap(lambda own: jnp.searchsorted(jnp.cumsum(ragged(own, N_CTX // 2, SEQ, 4 * TOK_DEV, 1)), jnp.arange(SEQ), side="right"))(jax.random.split(splits[5], BATCH)).reshape((BATCH, SEQ)).astype(jnp.int32),
        "member_rank": draw_member_rank(jax.random.fold_in(splits[8], 71), 0),
        "take_count": draw_take_count(jax.random.fold_in(splits[8], 71), 0),
    }


def rounded(tensor):
    return lax.optimization_barrier(tensor.astype(jnp.bfloat16)).astype(jnp.float32)

def member_layout(member_rank, take_count):
    cycle_size = member_rank.shape[0]
    block_rows = TOK_DEV
    spare_rows = TOK_DEV // 4
    member_indices = jnp.arange(cycle_size, dtype=jnp.int32)
    excluded = jnp.sum(jnp.where(member_rank < 0, member_indices, 0)).astype(jnp.int32)
    starts = (jnp.cumsum(take_count) - take_count).astype(jnp.int32)
    members = jnp.arange(cycle_size - 1, dtype=jnp.int32)
    owners = members + (members >= excluded).astype(jnp.int32)
    spare_ids = jnp.arange(spare_rows, dtype=jnp.int32)
    own_rows = owners[:, None] * block_rows + jnp.arange(block_rows, dtype=jnp.int32)[None, :]
    taken_rows = excluded * block_rows + starts[owners][:, None] + spare_ids[None, :]
    all_rows = jnp.concatenate([own_rows, taken_rows], 1)
    is_live = jnp.concatenate([jnp.ones((cycle_size - 1, block_rows), dtype=bool), spare_ids[None, :] < take_count[owners][:, None]], 1)
    return (jnp.minimum(all_rows, SEQ - 1).astype(jnp.int32), is_live)

def sequence_grads(query_seq, key_seq, value_seq, upstream_seq, doc_seq, all_rows, is_live):
    group_size = H // KVH
    score_scale = 1.0 / math.sqrt(HD)
    ext_rows = all_rows.shape[1]
    member_total = all_rows.shape[0]

    def member_step(carry, position):
        grad_q_acc, grad_k_acc, grad_v_acc = carry
        query_rows = all_rows[position]
        query_live = is_live[position]
        key_list = []
        live_list = []
        for offset in range(3):
            earlier = position - offset
            clipped = jnp.maximum(earlier, 0)
            key_list.append(all_rows[clipped])
            live_list.append(is_live[clipped] & (earlier >= 0))
        key_rows = jnp.concatenate(key_list)
        key_live = jnp.concatenate(live_list)
        q_block = query_seq[query_rows].astype(jnp.float32).reshape(ext_rows, KVH, group_size, HD)
        g_block = upstream_seq[query_rows].astype(jnp.float32).reshape(ext_rows, KVH, group_size, HD)
        k_block = key_seq[key_rows].astype(jnp.float32).reshape(3 * ext_rows, KVH, HD)
        v_block = value_seq[key_rows].astype(jnp.float32).reshape(3 * ext_rows, KVH, HD)
        visible = query_live[:, None] & key_live[None, :] & (doc_seq[query_rows][:, None] == doc_seq[key_rows][None, :]) & (key_rows[None, :] <= query_rows[:, None])
        scores = jnp.einsum('iagd,jad->agij', q_block, k_block) * score_scale
        pushes = jnp.einsum('iagd,jad->agij', g_block, v_block)
        row_max = lax.optimization_barrier(jnp.max(jnp.where(visible, scores, -1e+30), -1, keepdims=True))
        weights = jnp.where(visible, jnp.exp(scores - row_max), 0.0)
        row_total = jnp.where(query_live[:, None], lax.optimization_barrier(jnp.sum(weights, -1, keepdims=True)), 1.0)
        prob_rows = weights / row_total
        row_delta = lax.optimization_barrier(jnp.sum(prob_rows * pushes, -1, keepdims=True))
        dscore_b = rounded(prob_rows * (pushes - row_delta))
        probs_b = rounded(prob_rows)
        grad_q_rows = jnp.einsum('agij,jad->iagd', dscore_b, k_block) * score_scale
        grad_k_rows = jnp.einsum('agij,iagd->jad', dscore_b, q_block) * score_scale
        grad_v_rows = jnp.einsum('agij,iagd->jad', probs_b, g_block)
        grad_q_acc = grad_q_acc.at[query_rows].add(grad_q_rows.reshape(ext_rows, H * HD))
        grad_k_acc = grad_k_acc.at[key_rows].add(grad_k_rows.reshape(3 * ext_rows, KVH * HD))
        grad_v_acc = grad_v_acc.at[key_rows].add(grad_v_rows.reshape(3 * ext_rows, KVH * HD))
        return ((grad_q_acc, grad_k_acc, grad_v_acc), None)
    start_carry = (jnp.zeros((SEQ, H * HD), jnp.float32), jnp.zeros((SEQ, KVH * HD), jnp.float32), jnp.zeros((SEQ, KVH * HD), jnp.float32))
    final_carry, unused = lax.scan(member_step, start_carry, jnp.arange(member_total, dtype=jnp.int32))
    return final_carry

def reference(queries, keys, values, grad_out, layer_inputs, doc_ids, member_rank, take_count):
    all_rows, is_live = member_layout(member_rank, take_count)
    out_q = []
    out_k = []
    out_v = []
    weight_grad = jnp.zeros((D, 2, KVH * HD), jnp.float32)
    for sequence in range(BATCH):
        grad_q_acc, grad_k_acc, grad_v_acc = sequence_grads(queries[sequence], keys[sequence], values[sequence], grad_out[sequence], doc_ids[sequence], all_rows, is_live)
        grad_q_seq = grad_q_acc.astype(jnp.bfloat16)
        grad_k_seq = grad_k_acc.astype(jnp.bfloat16)
        grad_v_seq = grad_v_acc.astype(jnp.bfloat16)
        inputs_t = layer_inputs[sequence].T
        weight_grad = weight_grad + jnp.stack([jnp.dot(inputs_t, grad_k_seq, preferred_element_type=jnp.float32), jnp.dot(inputs_t, grad_v_seq, preferred_element_type=jnp.float32)], 1)
        out_q.append(grad_q_seq)
        out_k.append(grad_k_seq)
        out_v.append(grad_v_seq)
    return (jnp.stack(out_q), jnp.stack(out_k), jnp.stack(out_v), weight_grad)
```

```python
import math

import jax
import jax.numpy as jnp
from jax import lax
from jax.experimental import pallas as pl
from jax.experimental.pallas import tpu as pltpu
from jax.sharding import PartitionSpec as P

HD = 128
BLK = 128
NCTX = 16
NZ = 8
NY = 4
NH = 8
GROUP = 8
WIN = 640
ROWS = 160
BACK = 4
KEYS = (BACK + 1) * BLK
NEG = -1e30
SCALE = 1.0 / math.sqrt(HD)
MESH = pl.DeviceIdType.MESH


def dot(a, b, dims):
    return lax.dot_general(a, b, (dims, ((), ())), preferred_element_type=jnp.float32)


def kernel(
    q_hbm, k_hbm, v_hbm, g_hbm, x_hbm, doc_ref, rank_ref, take_ref,
    oq_hbm, ok_ref, ov_ref, ow_ref,
    qbuf, gbuf, kall, vall, bias, dsb, pbb, csend, crecv, dq, xall, xt, gall, acc, e1, u2, e2,
    loc_sem, a_send, a_recv, x1_send, x1_recv, x2_send, x2_recv, x3_send, x3_recv,
    c_send, c_recv, d_send, d_recv, e_send, e_recv,
):
    c = lax.axis_index("ctx")
    h = lax.axis_index("head")
    d = lax.axis_index("dp")
    z, xl = c // 2, c % 2
    xh, y = h // NY, h % NY

    def ctx(delta):
        return {"ctx": (c + delta + NCTX) % NCTX}

    def head(dx, dy):
        return {"head": ((xh + dx) % 2) * NY + (y + dy) % NY}

    x_peer = {"ctx": c + 1 - 2 * xl}
    core_peer = {"dp": 1 - d}

    local = []

    def fetch(src, dst):
        copy = pltpu.make_async_copy(src, dst, loc_sem.at[len(local)])
        copy.start()
        local.append(copy)

    fetch(k_hbm, kall.at[pl.ds(0, BLK)])
    fetch(v_hbm, vall.at[pl.ds(0, BLK)])
    for n in range(GROUP):
        fetch(q_hbm.at[:, pl.ds(n * HD, HD)], qbuf.at[pl.ds(n * BLK, BLK)])
        fetch(g_hbm.at[:, pl.ds(n * HD, HD)], gbuf.at[pl.ds(n * BLK, BLK)])
    fetch(x_hbm.at[:, pl.ds(pl.multiple_of(z * WIN, 128), WIN)], xall.at[z, h])

    barrier = pltpu.get_barrier_semaphore()
    peers = [ctx(s) for s in (1, 2, 3, 4, -1, -2, -3, -4, 6, -6, 8)]
    peers += [head(1, 0), head(0, 1), head(0, 2), head(0, 3), core_peer]
    for peer in peers:
        pl.semaphore_signal(barrier, inc=1, device_id=peer, device_id_type=MESH)
    pl.semaphore_wait(barrier, len(peers))

    def push(src, dst, send, recv, peer):
        copy = pltpu.make_async_remote_copy(
            src_ref=src, dst_ref=dst, send_sem=send, recv_sem=recv,
            device_id=peer, device_id_type=MESH,
        )
        copy.start()
        return copy

    a_copies = []
    for j in range(1, BACK + 1):
        rows = pl.ds(j * BLK, BLK)
        i = 2 * (j - 1)
        a_copies.append(push(k_hbm, kall.at[rows], a_send.at[i], a_recv.at[i], ctx(j)))
        a_copies.append(
            push(v_hbm, vall.at[rows], a_send.at[i + 1], a_recv.at[i + 1], ctx(j))
        )
    x1_copies = []
    for s in range(1, NZ):
        there = (z + s) % NZ
        x1_copies.append(
            push(
                x_hbm.at[:, pl.ds(pl.multiple_of(there * WIN, 128), WIN)],
                xall.at[z, h], x1_send.at[s - 1], x1_recv.at[s - 1], ctx(2 * s),
            )
        )

    down = lax.broadcasted_iota(jnp.int32, (BLK, BLK), 0)
    across = lax.broadcasted_iota(jnp.int32, (BLK, BLK), 1)
    excluded = jnp.int32(0)
    end = jnp.int32(0)
    count_down = jnp.zeros((BLK, BLK), jnp.int32)
    count_across = jnp.zeros((BLK, BLK), jnp.int32)
    for b in range(NCTX):
        excluded = excluded + jnp.where(rank_ref[b] < 0, b, 0)
        end = end + take_ref[b]
        count_down = count_down + jnp.where(down >= end, 1, 0)
        count_across = count_across + jnp.where(across >= end, 1, 0)
    taken_down = count_down - jnp.where(count_down > excluded, 1, 0)
    taken_across = count_across - jnp.where(count_across > excluded, 1, 0)
    my_rank = jnp.full((BLK, BLK), rank_ref[c], jnp.int32)
    slot_t = jnp.where(my_rank < 0, taken_across, my_rank)
    doc_t = jnp.broadcast_to(
        doc_ref[:, pl.ds(pl.multiple_of(c * BLK, BLK), BLK)], (BLK, BLK)
    )
    for j in range(BACK + 1):
        b = (c - j + NCTX) % NCTX
        rank = jnp.full((BLK, BLK), rank_ref[b], jnp.int32)
        gap = slot_t - jnp.where(rank < 0, taken_down, rank)
        doc_u = jnp.broadcast_to(
            doc_ref[:, pl.ds(pl.multiple_of(b * BLK, BLK), BLK)], (BLK, BLK)
        ).T
        order = (c * BLK + across) - (b * BLK + down)
        seen = (doc_u == doc_t) & (order >= 0) & (gap >= 0) & (gap <= 2)
        bias[pl.ds(j * BLK, BLK), :] = jnp.where(seen, 0.0, NEG)

    for copy in local:
        copy.wait()
    for copy in a_copies:
        copy.wait_recv()
    for copy in x1_copies:
        copy.wait_recv()
    x2_copies = []
    for i, peer in enumerate([head(1, 0), head(0, 1), head(0, 2), head(0, 3)]):
        x2_copies.append(
            push(xall.at[:, h], xall.at[:, h], x2_send.at[i], x2_recv.at[i], peer)
        )

    def weigh(p, carry):
        cols = pl.ds(pl.multiple_of(p * 2 * BLK, 2 * BLK), 2 * BLK)
        q2, g2 = qbuf[cols, :], gbuf[cols, :]
        hidden = bias[...]
        scores = dot(kall[...], q2, ((1,), (1,))) * SCALE
        scores = scores + jnp.concatenate([hidden, hidden], 1)
        top = jnp.max(scores, 0, keepdims=True)
        weights = jnp.exp(scores - top)
        total = jnp.sum(weights, 0, keepdims=True)
        probs = weights * (1.0 / total)
        pushes = dot(vall[...], g2, ((1,), (1,)))
        delta = jnp.sum(probs * pushes, 0, keepdims=True)
        dsb[:, cols] = (probs * (pushes - delta)).astype(jnp.bfloat16)
        pbb[:, cols] = probs.astype(jnp.bfloat16)
        return carry

    lax.fori_loop(0, GROUP // 2, weigh, 0)

    def key_grads(j):
        rows = pl.ds(j * BLK, BLK)
        grad_k = dot(dsb[rows, :], qbuf[...], ((1,), (0,))) * SCALE
        grad_v = dot(pbb[rows, :], gbuf[...], ((1,), (0,)))
        return grad_k, grad_v

    c_copies = []
    for j in range(BACK, 0, -1):
        grad_k, grad_v = key_grads(j)
        csend[j - 1, :, :HD] = grad_k.astype(jnp.bfloat16)
        csend[j - 1, :, HD:] = grad_v.astype(jnp.bfloat16)
        c_copies.append(
            push(
                csend.at[j - 1], crecv.at[j - 1], c_send.at[j - 1], c_recv.at[j - 1], ctx(-j)
            )
        )
    x2_copies[0].wait_recv()
    other = (1 - xh) * NY + y
    x3_copies = []
    for i in range(NY - 1):
        x3_copies.append(
            push(
                xall.at[:, other], xall.at[:, other],
                x3_send.at[i], x3_recv.at[i], head(0, i + 1),
            )
        )
    own_k, own_v = key_grads(0)

    def query_grads(p, carry):
        cols = pl.ds(pl.multiple_of(p * 2 * BLK, 2 * BLK), 2 * BLK)
        both = dot(dsb[:, cols], kall[...], ((0,), (0,))) * SCALE
        dq[2 * p] = both[:BLK].astype(jnp.bfloat16)
        dq[2 * p + 1] = both[BLK:].astype(jnp.bfloat16)
        return carry

    lax.fori_loop(0, GROUP // 2, query_grads, 0)
    out_copies = []
    for n in range(GROUP):
        copy = pltpu.make_async_copy(
            dq.at[n], oq_hbm.at[:, pl.ds(n * HD, HD)], loc_sem.at[n]
        )
        copy.start()
        out_copies.append(copy)

    for copy in x2_copies[1:]:
        copy.wait_recv()
    for copy in x3_copies:
        copy.wait_recv()

    def flip(s, carry):
        xt[s] = xall[s].reshape(BLK, WIN).T
        return carry

    lax.fori_loop(0, NZ, flip, 0)

    for copy in c_copies:
        copy.wait_recv()
    for j in range(BACK):
        own_k = own_k + crecv[j, :, :HD].astype(jnp.float32)
        own_v = own_v + crecv[j, :, HD:].astype(jnp.float32)
    final_k, final_v = own_k.astype(jnp.bfloat16), own_v.astype(jnp.bfloat16)
    gall[z, :, :HD] = final_k
    gall[z, :, HD:] = final_v
    ok_ref[...] = final_k
    ov_ref[...] = final_v

    def relay(step):
        up, low = (z - step + NZ) % NZ, (z + step) % NZ
        if step < NZ // 2 - 1:
            part_up, part_low = gall.at[up], gall.at[low]
        else:
            part_up = gall.at[up, :, pl.ds(0, HD)]
            part_low = gall.at[low, :, pl.ds(HD, HD)]
        return (
            push(part_up, part_up, d_send.at[0, step], d_recv.at[0, step], ctx(2)),
            push(part_low, part_low, d_send.at[1, step], d_recv.at[1, step], ctx(-2)),
        )

    d_copies = [relay(0)]
    acc[...] = dot(xt[z], gall[z], ((1,), (0,)))
    for step in range(1, NZ // 2 + 1):
        for copy in d_copies[-1]:
            copy.wait_recv()
        if step < NZ // 2:
            d_copies.append(relay(step))
        up, low = (z - step + NZ) % NZ, (z + step) % NZ
        if step < NZ // 2:
            acc[...] += dot(xt[up], gall[up], ((1,), (0,))) + dot(
                xt[low], gall[low], ((1,), (0,))
            )
        else:
            acc[...] += dot(xt[up], gall[up], ((1,), (0,)))

    def part(side, core):
        return pl.ds(pl.multiple_of(side * 2 * ROWS + core * ROWS, 32), ROWS)

    e_copies = []
    for i, side in enumerate((1 - xl, xl)):
        e_copies.append(
            push(acc.at[part(side, 1 - d)], e1.at[i], e_send.at[i], e_recv.at[i], core_peer)
        )
    e_copies[0].wait_recv()
    u2[...] = acc[part(1 - xl, d), :] + e1[0]
    e_copies.append(push(u2, e2, e_send.at[2], e_recv.at[2], x_peer))
    e_copies[1].wait_recv()
    e_copies[2].wait_recv()
    ow_ref[...] = acc[part(xl, d), :] + e1[1] + e2[...]

    for copy in out_copies:
        copy.wait()
    for copy in a_copies + x1_copies + x2_copies + x3_copies + c_copies + e_copies:
        copy.wait_send()
    for pair in d_copies:
        for copy in pair:
            copy.wait_send()


def local(queries, keys, values, grad_out, layer_inputs, doc_ids, member_rank, take_count):
    bf16, f32 = jnp.bfloat16, jnp.float32
    hbm = pl.BlockSpec(memory_space=pl.ANY)
    vmem = pl.BlockSpec(memory_space=pltpu.VMEM)
    smem = pl.BlockSpec(memory_space=pltpu.SMEM)
    dma = pltpu.SemaphoreType.DMA
    grad_q, grad_k, grad_v, grad_w = pl.pallas_call(
        kernel,
        out_shape=[
            jax.ShapeDtypeStruct((BLK, GROUP * HD), bf16),
            jax.ShapeDtypeStruct((BLK, HD), bf16),
            jax.ShapeDtypeStruct((BLK, HD), bf16),
            jax.ShapeDtypeStruct((ROWS, 2 * HD), f32),
        ],
        in_specs=[hbm] * 5 + [vmem, smem, smem],
        out_specs=[hbm, vmem, vmem, vmem],
        scratch_shapes=[
            pltpu.VMEM((GROUP * BLK, HD), bf16),
            pltpu.VMEM((GROUP * BLK, HD), bf16),
            pltpu.VMEM((KEYS, HD), bf16),
            pltpu.VMEM((KEYS, HD), bf16),
            pltpu.VMEM((KEYS, BLK), f32),
            pltpu.VMEM((KEYS, GROUP * BLK), bf16),
            pltpu.VMEM((KEYS, GROUP * BLK), bf16),
            pltpu.VMEM((BACK, BLK, 2 * HD), bf16),
            pltpu.VMEM((BACK, BLK, 2 * HD), bf16),
            pltpu.VMEM((GROUP, BLK, HD), bf16),
            pltpu.VMEM((NZ, NH, BLK // NH, WIN), bf16),
            pltpu.VMEM((NZ, WIN, BLK), bf16),
            pltpu.VMEM((NZ, BLK, 2 * HD), bf16),
            pltpu.VMEM((WIN, 2 * HD), f32),
            pltpu.VMEM((2, ROWS, 2 * HD), f32),
            pltpu.VMEM((ROWS, 2 * HD), f32),
            pltpu.VMEM((ROWS, 2 * HD), f32),
            dma((2 * GROUP + 3,)),
            dma((2 * BACK,)),
            dma((2 * BACK,)),
            dma((NZ - 1,)),
            dma((NZ - 1,)),
            dma((NY,)),
            dma((NY,)),
            dma((NY - 1,)),
            dma((NY - 1,)),
            dma((BACK,)),
            dma((BACK,)),
            dma((2, NZ // 2)),
            dma((2, NZ // 2)),
            dma((3,)),
            dma((3,)),
        ],
        compiler_params=pltpu.CompilerParams(
            collective_id=0, has_side_effects=True, vmem_limit_bytes=40 * 1024 * 1024
        ),
        cost_estimate=pl.CostEstimate(
            flops=1300000000, bytes_accessed=2000000, transcendentals=700000
        ),
    )(
        queries[0], keys[0], values[0], grad_out[0], layer_inputs[0],
        doc_ids, member_rank, take_count,
    )
    return (grad_q[None], grad_k[None], grad_v[None], grad_w.reshape(ROWS, 2, HD))


def solution(mesh):
    in_specs = (
        P("dp", "ctx", "head"),
        P("dp", "ctx", "head"),
        P("dp", "ctx", "head"),
        P("dp", "ctx", "head"),
        P("dp", ("ctx", "head"), None),
        P("dp", None),
        P(),
        P(),
    )
    out_specs = (
        P("dp", "ctx", "head"),
        P("dp", "ctx", "head"),
        P("dp", "ctx", "head"),
        P(("ctx", "dp"), None, "head"),
    )
    return jax.shard_map(local, mesh=mesh, in_specs=in_specs, out_specs=out_specs, check_vma=False)
```

```python
import math

import jax
import jax.numpy as jnp
from jax import lax
from jax.experimental import pallas as pl
from jax.experimental.pallas import tpu as pltpu
from jax.sharding import PartitionSpec as P

HD = 128
BLK = 128
NCTX = 16
NZ = 8
NY = 4
NH = 8
GROUP = 8
WIN = 640
ROWS = 160
BACK = 4
KEYS = (BACK + 1) * BLK
NEG = -1e30
PLACE = (0, 1, 3, 5, 7, 6, 4, 2)
ORDER = (4, 3, 5, 2, 6, 1, 7)
SCALE = 1.0 / math.sqrt(HD)
MESH = pl.DeviceIdType.MESH


def dot(a, b, dims):
    return lax.dot_general(a, b, (dims, ((), ())), preferred_element_type=jnp.float32)


def kernel(
    q_hbm, k_hbm, v_hbm, g_hbm, x_hbm, doc_ref, rank_ref, take_ref,
    oq_ref, ok_ref, ov_ref, ow_ref,
    qbuf, gbuf, xbuf, kall, vall, bias, probs, dsb, pbb, vsend, vrecv, ksend, krecv,
    xall, xt, gv, gk, acc_v, acc_k, e1, u2, e2,
    loc_sem, a_send, a_recv, x1_send, x1_recv, x2_send, x2_recv,
    c_send, c_recv, d_send, d_recv, e_send, e_recv,
):
    c = lax.axis_index("ctx")
    h = lax.axis_index("head")
    d = lax.axis_index("dp")
    z, xl = c // 2, c % 2
    xh, y = h // NY, h % NY

    def ctx(delta):
        return {"ctx": (c + delta + NCTX) % NCTX}

    def head_index(dx, dy):
        return ((xh + dx) % 2) * NY + (y + dy + NY) % NY

    def head(dx, dy):
        return {"head": head_index(dx, dy)}

    x_peer = {"ctx": c + 1 - 2 * xl}
    core_peer = {"dp": 1 - d}

    barrier = pltpu.get_barrier_semaphore()
    peers = [ctx(s) for s in (1, 2, 3, 4, -1, -2, -3, -4, 6, -6, 8)]
    peers += [head(1, 0), head(0, 1), head(0, 2), head(0, 3), core_peer]
    for peer in peers:
        pl.semaphore_signal(barrier, inc=1, device_id=peer, device_id_type=MESH)

    local = []

    def fetch(src, dst):
        copy = pltpu.make_async_copy(src, dst, loc_sem.at[len(local)])
        copy.start()
        local.append(copy)

    fetch(k_hbm, kall.at[pl.ds(0, BLK)])
    fetch(v_hbm, vall.at[pl.ds(0, BLK)])
    fetch(x_hbm, xbuf)
    for n in range(GROUP):
        fetch(q_hbm.at[:, pl.ds(n * HD, HD)], qbuf.at[pl.ds(n * BLK, BLK)])
        fetch(g_hbm.at[:, pl.ds(n * HD, HD)], gbuf.at[pl.ds(n * BLK, BLK)])

    down = lax.broadcasted_iota(jnp.int32, (BLK, BLK), 0)
    across = lax.broadcasted_iota(jnp.int32, (BLK, BLK), 1)
    excluded = jnp.int32(0)
    end = jnp.int32(0)
    count_down = jnp.zeros((BLK, BLK), jnp.int32)
    count_across = jnp.zeros((BLK, BLK), jnp.int32)
    for b in range(NCTX):
        excluded = excluded + jnp.where(rank_ref[b] < 0, b, 0)
        end = end + take_ref[b]
        count_down = count_down + jnp.where(down >= end, 1, 0)
        count_across = count_across + jnp.where(across >= end, 1, 0)
    taken_down = count_down - jnp.where(count_down > excluded, 1, 0)
    taken_across = count_across - jnp.where(count_across > excluded, 1, 0)
    my_rank = jnp.full((BLK, BLK), rank_ref[c], jnp.int32)
    slot_t = jnp.where(my_rank < 0, taken_across, my_rank)
    doc_t = jnp.broadcast_to(
        doc_ref[:, pl.ds(pl.multiple_of(c * BLK, BLK), BLK)], (BLK, BLK)
    )
    for j in range(BACK + 1):
        b = (c - j + NCTX) % NCTX
        rank = jnp.full((BLK, BLK), rank_ref[b], jnp.int32)
        gap = slot_t - jnp.where(rank < 0, taken_down, rank)
        doc_u = jnp.broadcast_to(
            doc_ref[:, pl.ds(pl.multiple_of(b * BLK, BLK), BLK)], (BLK, BLK)
        ).T
        order = (c * BLK + across) - (b * BLK + down)
        seen = (doc_u == doc_t) & (order >= 0) & (gap >= 0) & (gap <= 2)
        bias[pl.ds(j * BLK, BLK), :] = jnp.where(seen, 0.0, NEG)

    for copy in local:
        copy.wait()
    window = xbuf[:, pl.ds(pl.multiple_of(z * WIN, 128), WIN)]
    xall[0, h] = window
    pl.semaphore_wait(barrier, len(peers))

    def push(src, dst, send, recv, peer):
        copy = pltpu.make_async_remote_copy(
            src_ref=src, dst_ref=dst, send_sem=send, recv_sem=recv,
            device_id=peer, device_id_type=MESH,
        )
        copy.start()
        return copy

    a_copies = []
    for kind, held in enumerate((kall, vall)):
        for j in range(BACK, 0, -1):
            a_copies.append(
                push(
                    held.at[pl.ds(0, BLK)], held.at[pl.ds(j * BLK, BLK)],
                    a_send.at[kind, j - 1], a_recv.at[kind, j - 1], ctx(j),
                )
            )
    x1_copies = []
    for s in range(1, NZ):
        there = (z + s) % NZ
        x1_copies.append(
            push(
                xbuf.at[:, pl.ds(pl.multiple_of(there * WIN, 128), WIN)],
                xall.at[PLACE[s], h], x1_send.at[s - 1], x1_recv.at[s - 1], ctx(2 * s),
            )
        )
    x2_copies = []

    def spread(at, peer):
        i = len(x2_copies)
        x2_copies.append(push(xall.at[:, at], xall.at[:, at], x2_send.at[i], x2_recv.at[i], peer))

    for copy in a_copies[:BACK]:
        copy.wait_recv()

    def weigh(p, carry):
        cols = pl.ds(pl.multiple_of(p * 2 * BLK, 2 * BLK), 2 * BLK)
        hidden = bias[...]
        scores = dot(kall[...], qbuf[cols, :], ((1,), (1,))) * SCALE
        scores = scores + jnp.concatenate([hidden, hidden], 1)
        top = jnp.max(scores, 0, keepdims=True)
        weights = jnp.exp(scores - top)
        total = jnp.sum(weights, 0, keepdims=True)
        share = weights * (1.0 / total)
        probs[:, cols] = share
        pbb[:, cols] = share.astype(jnp.bfloat16)
        return carry

    lax.fori_loop(0, GROUP // 2, weigh, 0)
    c_copies = []
    for j in range(BACK, 0, -1):
        grad_v = dot(pbb[pl.ds(j * BLK, BLK), :], gbuf[...], ((1,), (0,)))
        vsend[j - 1] = grad_v.astype(jnp.bfloat16)
        c_copies.append(
            push(
                vsend.at[j - 1], vrecv.at[j - 1],
                c_send.at[0, j - 1], c_recv.at[0, j - 1], ctx(-j),
            )
        )
    own_v = dot(pbb[pl.ds(0, BLK), :], gbuf[...], ((1,), (0,)))

    for copy in x1_copies:
        copy.wait_recv()
    spread(h, head(0, 1))
    spread(h, head(0, -1))
    spread(h, head(1, 0))

    for copy in a_copies[BACK:]:
        copy.wait_recv()

    def differ(p, carry):
        cols = pl.ds(pl.multiple_of(p * 2 * BLK, 2 * BLK), 2 * BLK)
        pushes = dot(vall[...], gbuf[cols, :], ((1,), (1,)))
        share = probs[:, cols]
        delta = jnp.sum(share * pushes, 0, keepdims=True)
        dsb[:, cols] = (share * (pushes - delta)).astype(jnp.bfloat16)
        return carry

    lax.fori_loop(0, GROUP // 2, differ, 0)
    for j in range(BACK, 0, -1):
        grad_k = dot(dsb[pl.ds(j * BLK, BLK), :], qbuf[...], ((1,), (0,))) * SCALE
        ksend[j - 1] = grad_k.astype(jnp.bfloat16)
        c_copies.append(
            push(
                ksend.at[j - 1], krecv.at[j - 1],
                c_send.at[1, j - 1], c_recv.at[1, j - 1], ctx(-j),
            )
        )
    own_k = dot(dsb[pl.ds(0, BLK), :], qbuf[...], ((1,), (0,))) * SCALE

    x2_copies[0].wait_recv()
    spread(head_index(0, -1), head(0, 1))

    d_copies = []

    def collect(kind, own, received, copies, held, out_ref):
        for copy in copies:
            copy.wait_recv()
        for j in range(BACK):
            own = own + received[j].astype(jnp.float32)
        final = own.astype(jnp.bfloat16)
        held[0] = final
        out_ref[...] = final
        for s in ORDER:
            d_copies.append(
                push(
                    held.at[0], held.at[PLACE[s]],
                    d_send.at[kind, s - 1], d_recv.at[kind, s - 1], ctx(2 * s),
                )
            )

    collect(0, own_v, vrecv, c_copies[:BACK], gv, ov_ref)

    def query_grads(p, carry):
        cols = pl.ds(pl.multiple_of(p * 2 * BLK, 2 * BLK), 2 * BLK)
        both = dot(dsb[:, cols], kall[...], ((0,), (0,))) * SCALE
        both = both.astype(jnp.bfloat16)
        oq_ref[:, cols] = jnp.concatenate([both[:BLK], both[BLK:]], 1)
        return carry

    lax.fori_loop(0, GROUP // 2, query_grads, 0)

    x2_copies[2].wait_recv()
    spread(head_index(1, 0), head(0, 1))
    spread(head_index(1, 0), head(0, -1))

    collect(1, own_k, krecv, c_copies[BACK:], gk, ok_ref)

    x2_copies[5].wait_recv()
    spread(head_index(1, 1), head(0, -1))
    for i in (1, 3, 4, 6):
        x2_copies[i].wait_recv()

    for i in range(NZ):
        xt[:, pl.ds(i * BLK, BLK)] = xall[i].reshape(BLK, WIN).T

    e_copies = []

    def reduce_cores(kind, held, acc):
        for copy in d_copies[kind * (NZ - 1) : (kind + 1) * (NZ - 1)]:
            copy.wait_recv()
        product = dot(xt[...], held[...].reshape(NZ * BLK, HD), ((1,), (0,)))
        acc[...] = product.reshape(2, 2, ROWS, HD)
        e_copies.append(
            push(
                acc.at[:, 1 - d], e1.at[kind],
                e_send.at[0, kind], e_recv.at[0, kind], core_peer,
            )
        )
        e_copies[-1].wait_recv()
        u2[kind] = acc[1 - xl, d] + e1[kind, 1 - xl]
        e_copies.append(
            push(
                u2.at[kind], e2.at[kind],
                e_send.at[1, kind], e_recv.at[1, kind], x_peer,
            )
        )

    reduce_cores(0, gv, acc_v)
    reduce_cores(1, gk, acc_k)
    e_copies[1].wait_recv()
    ow_ref[1] = acc_v[xl, d] + e1[0, xl] + e2[0]
    e_copies[3].wait_recv()
    ow_ref[0] = acc_k[xl, d] + e1[1, xl] + e2[1]

    for copy in a_copies + x1_copies + x2_copies + c_copies + d_copies + e_copies:
        copy.wait_send()


def finish(q_ref, k_ref, v_ref, w_ref, oq_ref, ok_ref, ov_ref, ow_ref):
    oq_ref[...] = q_ref[...]
    ok_ref[...] = k_ref[...]
    ov_ref[...] = v_ref[...]
    ow_ref[:, 0, :] = w_ref[0]
    ow_ref[:, 1, :] = w_ref[1]


def local(queries, keys, values, grad_out, layer_inputs, doc_ids, member_rank, take_count):
    bf16, f32 = jnp.bfloat16, jnp.float32
    hbm = pl.BlockSpec(memory_space=pltpu.HBM)
    vmem = pl.BlockSpec(memory_space=pltpu.VMEM)
    smem = pl.BlockSpec(memory_space=pltpu.SMEM)
    dma = pltpu.SemaphoreType.DMA
    grad_q, grad_k, grad_v, grad_w = pl.pallas_call(
        kernel,
        out_shape=[
            jax.ShapeDtypeStruct((BLK, GROUP * HD), bf16),
            jax.ShapeDtypeStruct((BLK, HD), bf16),
            jax.ShapeDtypeStruct((BLK, HD), bf16),
            jax.ShapeDtypeStruct((2, ROWS, HD), f32),
        ],
        in_specs=[hbm] * 5 + [vmem, smem, smem],
        out_specs=[vmem] * 4,
        scratch_shapes=[
            pltpu.VMEM((GROUP * BLK, HD), bf16),
            pltpu.VMEM((GROUP * BLK, HD), bf16),
            pltpu.VMEM((BLK // NH, NZ * WIN), bf16),
            pltpu.VMEM((KEYS, HD), bf16),
            pltpu.VMEM((KEYS, HD), bf16),
            pltpu.VMEM((KEYS, BLK), f32),
            pltpu.VMEM((KEYS, GROUP * BLK), f32),
            pltpu.VMEM((KEYS, GROUP * BLK), bf16),
            pltpu.VMEM((KEYS, GROUP * BLK), bf16),
            pltpu.VMEM((BACK, BLK, HD), bf16),
            pltpu.VMEM((BACK, BLK, HD), bf16),
            pltpu.VMEM((BACK, BLK, HD), bf16),
            pltpu.VMEM((BACK, BLK, HD), bf16),
            pltpu.VMEM((NZ, NH, BLK // NH, WIN), bf16),
            pltpu.VMEM((WIN, NZ * BLK), bf16),
            pltpu.VMEM((NZ, BLK, HD), bf16),
            pltpu.VMEM((NZ, BLK, HD), bf16),
            pltpu.VMEM((2, 2, ROWS, HD), f32),
            pltpu.VMEM((2, 2, ROWS, HD), f32),
            pltpu.VMEM((2, 2, ROWS, HD), f32),
            pltpu.VMEM((2, ROWS, HD), f32),
            pltpu.VMEM((2, ROWS, HD), f32),
            dma((2 * GROUP + 3,)),
            dma((2, BACK)),
            dma((2, BACK)),
            dma((NZ - 1,)),
            dma((NZ - 1,)),
            dma((7,)),
            dma((7,)),
            dma((2, BACK)),
            dma((2, BACK)),
            dma((2, NZ - 1)),
            dma((2, NZ - 1)),
            dma((2, 2)),
            dma((2, 2)),
        ],
        compiler_params=pltpu.CompilerParams(
            collective_id=0, has_side_effects=True, vmem_limit_bytes=60 * 1024 * 1024
        ),
        cost_estimate=pl.CostEstimate(
            flops=1300000000, bytes_accessed=2000000, transcendentals=700000
        ),
    )(
        queries[0], keys[0], values[0], grad_out[0], layer_inputs[0],
        doc_ids, member_rank, take_count,
    )
    grad_q, grad_k, grad_v, grad_w = pl.pallas_call(
        finish,
        out_shape=[
            jax.ShapeDtypeStruct((BLK, GROUP * HD), bf16),
            jax.ShapeDtypeStruct((BLK, HD), bf16),
            jax.ShapeDtypeStruct((BLK, HD), bf16),
            jax.ShapeDtypeStruct((ROWS, 2, HD), f32),
        ],
        in_specs=[vmem] * 4,
        out_specs=[vmem] * 4,
    )(grad_q, grad_k, grad_v, grad_w)
    return (grad_q[None], grad_k[None], grad_v[None], grad_w)


def solution(mesh):
    in_specs = (
        P("dp", "ctx", "head"),
        P("dp", "ctx", "head"),
        P("dp", "ctx", "head"),
        P("dp", "ctx", "head"),
        P("dp", ("ctx", "head"), None),
        P("dp", None),
        P(),
        P(),
    )
    out_specs = (
        P("dp", "ctx", "head"),
        P("dp", "ctx", "head"),
        P("dp", "ctx", "head"),
        P(("ctx", "dp"), None, "head"),
    )
    return jax.shard_map(local, mesh=mesh, in_specs=in_specs, out_specs=out_specs, check_vma=False)
```

```python
import math

import jax
import jax.numpy as jnp
from jax import lax
from jax.experimental import pallas as pl
from jax.experimental.pallas import tpu as pltpu
from jax.sharding import PartitionSpec as P

HD = 128
BLK = 128
NCTX = 16
NZ = 8
NY = 4
NH = 8
GROUP = 8
WIN = 1280
ROWS = 160
BACK = 4
KEYS = (BACK + 1) * BLK
NEG = -1e30
TERMS = 4
SCALE = 1.0 / math.sqrt(HD)
MESH = pl.DeviceIdType.MESH


def dot(a, b, dims):
    return lax.dot_general(a, b, (dims, ((), ())), preferred_element_type=jnp.float32)


def kernel(
    q_hbm, k_hbm, v_hbm, g_hbm, x_hbm, doc_ref, rank_ref, take_ref,
    oq_ref, ok_ref, ov_ref, ow_ref,
    qbuf, gbuf, xbuf, kall, vall, bias, probs, dsb, pbb, vsend, vrecv, ksend, krecv,
    xall, xt, gv, gk, acc_v, acc_k, e1, u2, e2,
    loc_sem, a_send, a_recv, x1_send, x1_recv, x2_send, x2_recv,
    c_send, c_recv, d_send, d_recv, e_send, e_recv,
):
    c = lax.axis_index("ctx")
    h = lax.axis_index("head")
    d = lax.axis_index("dp")
    z, xl = c // 2, c % 2
    xh, y = h // NY, h % NY
    side = z % 2
    way = 1 - 2 * side

    def ctx(delta):
        return {"ctx": (c + delta + NCTX) % NCTX}

    def head_index(dx, dy):
        return ((xh + dx) % 2) * NY + (y + dy + NY) % NY

    def head(dx, dy):
        return {"head": head_index(dx, dy)}

    core_peer = {"dp": 1 - d}
    side_peer = {"ctx": c + 2 * way}
    x_peer = {"ctx": c + 1 - 2 * xl}
    far_peer = {"ctx": c + 2 * way + 1 - 2 * xl}
    reach = {1: -way, 2: 2 * way, 3: -3 * way}

    barrier = pltpu.get_barrier_semaphore()
    peers = [ctx(s) for s in (1, 2, 3, 4, -1, -2, -3, -4)] + [ctx(-6 * way)]
    peers += [head(1, 0), head(0, 1), head(0, 2), head(0, 3), core_peer]
    for peer in peers:
        pl.semaphore_signal(barrier, inc=1, device_id=peer, device_id_type=MESH)

    local = []

    def fetch(src, dst):
        copy = pltpu.make_async_copy(src, dst, loc_sem.at[len(local)])
        copy.start()
        local.append(copy)

    fetch(k_hbm, kall.at[pl.ds(0, BLK)])
    fetch(v_hbm, vall.at[pl.ds(0, BLK)])
    fetch(x_hbm, xbuf)
    for n in range(GROUP):
        fetch(q_hbm.at[:, pl.ds(n * HD, HD)], qbuf.at[pl.ds(n * BLK, BLK)])
        fetch(g_hbm.at[:, pl.ds(n * HD, HD)], gbuf.at[pl.ds(n * BLK, BLK)])

    down = lax.broadcasted_iota(jnp.int32, (BLK, BLK), 0)
    across = lax.broadcasted_iota(jnp.int32, (BLK, BLK), 1)
    excluded = jnp.int32(0)
    end = jnp.int32(0)
    count_down = jnp.zeros((BLK, BLK), jnp.int32)
    count_across = jnp.zeros((BLK, BLK), jnp.int32)
    for b in range(NCTX):
        excluded = excluded + jnp.where(rank_ref[b] < 0, b, 0)
        end = end + take_ref[b]
        count_down = count_down + jnp.where(down >= end, 1, 0)
        count_across = count_across + jnp.where(across >= end, 1, 0)
    taken_down = count_down - jnp.where(count_down > excluded, 1, 0)
    taken_across = count_across - jnp.where(count_across > excluded, 1, 0)
    my_rank = jnp.full((BLK, BLK), rank_ref[c], jnp.int32)
    slot_t = jnp.where(my_rank < 0, taken_across, my_rank)
    doc_t = jnp.broadcast_to(
        doc_ref[:, pl.ds(pl.multiple_of(c * BLK, BLK), BLK)], (BLK, BLK)
    )
    for j in range(BACK + 1):
        b = (c - j + NCTX) % NCTX
        rank = jnp.full((BLK, BLK), rank_ref[b], jnp.int32)
        gap = slot_t - jnp.where(rank < 0, taken_down, rank)
        doc_u = jnp.broadcast_to(
            doc_ref[:, pl.ds(pl.multiple_of(b * BLK, BLK), BLK)], (BLK, BLK)
        ).T
        order = (c * BLK + across) - (b * BLK + down)
        seen = (doc_u == doc_t) & (order >= 0) & (gap >= 0) & (gap <= 2)
        bias[pl.ds(j * BLK, BLK), :] = jnp.where(seen, 0.0, NEG)

    for copy in local:
        copy.wait()
    xall[0, h] = xbuf[:, pl.ds(pl.multiple_of((z // 2) * WIN, 128), WIN)]
    pl.semaphore_wait(barrier, len(peers))

    def push(src, dst, send, recv, peer):
        copy = pltpu.make_async_remote_copy(
            src_ref=src, dst_ref=dst, send_sem=send, recv_sem=recv,
            device_id=peer, device_id_type=MESH,
        )
        copy.start()
        return copy

    a_copies = {}

    def hand_on(kind, held, j, source, peer):
        a_copies[kind, j] = push(
            held.at[pl.ds(source, BLK)], held.at[pl.ds(j * BLK, BLK)],
            a_send.at[kind, j - 1], a_recv.at[kind, j - 1], peer,
        )

    hand_on(0, kall, 4, 0, ctx(4))
    hand_on(1, vall, 4, 0, ctx(4))
    hand_on(0, kall, 2, 0, ctx(2))
    hand_on(0, kall, 1, 0, ctx(1))
    x1_copies = []
    for r in (3, 2, 1):
        there = (z + reach[r] + NZ) % NZ // 2
        copy = push(
            xbuf.at[:, pl.ds(pl.multiple_of(there * WIN, 128), WIN)],
            xall.at[r, h], x1_send.at[r - 1], x1_recv.at[r - 1], ctx(2 * reach[r]),
        )
        x1_copies.append((r, copy))
    hand_on(1, vall, 2, 0, ctx(2))
    hand_on(1, vall, 1, 0, ctx(1))
    third = pl.multiple_of(xl * BACK * BLK, BLK)
    third_peer = {"ctx": (c + 3 - 4 * xl + NCTX) % NCTX}
    for kind, held in ((0, kall), (1, vall)):
        a_copies[kind, 4].wait_recv()
        hand_on(kind, held, 3, third, third_peer)
    x2_copies = {}

    def spread(step, group, at, peer):
        part = xall.at[pl.ds(2 * group, 2), at]
        x2_copies[step, group] = push(
            part, part, x2_send.at[group, step], x2_recv.at[group, step], peer
        )

    def spread_own(group):
        for copy in x1_copies:
            if copy[0] // 2 == group:
                copy[1].wait_recv()
        spread(0, group, h, head(1, 0))
        spread(1, group, h, head(0, 1))
        spread(2, group, h, head(0, -1))

    def spread_own_on(group):
        x2_copies[1, group].wait_recv()
        spread(3, group, head_index(0, -1), head(0, 1))

    def spread_other(group):
        x2_copies[0, group].wait_recv()
        spread(4, group, head_index(1, 0), head(0, 1))
        spread(5, group, head_index(1, 0), head(0, -1))

    def spread_other_on(group):
        x2_copies[5, group].wait_recv()
        spread(6, group, head_index(1, 1), head(0, -1))

    spread_own(0)
    spread_own(1)
    for j in (1, 2, 3):
        a_copies[0, j].wait_recv()

    def weigh(p, carry):
        cols = pl.ds(pl.multiple_of(p * 2 * BLK, 2 * BLK), 2 * BLK)
        hidden = bias[...]
        scores = dot(kall[...], qbuf[cols, :], ((1,), (1,))) * SCALE
        scores = scores + jnp.concatenate([hidden, hidden], 1)
        top = jnp.max(scores, 0, keepdims=True)
        weights = jnp.exp(scores - top)
        total = jnp.sum(weights, 0, keepdims=True)
        share = weights * (1.0 / total)
        probs[:, cols] = share
        pbb[:, cols] = share.astype(jnp.bfloat16)
        return carry

    lax.fori_loop(0, GROUP // 2, weigh, 0)
    c_copies = []
    for j in range(BACK, 0, -1):
        grad_v = dot(pbb[pl.ds(j * BLK, BLK), :], gbuf[...], ((1,), (0,)))
        vsend[j - 1] = grad_v.astype(jnp.bfloat16)
        c_copies.append(
            push(
                vsend.at[j - 1], vrecv.at[j - 1],
                c_send.at[0, j - 1], c_recv.at[0, j - 1], ctx(-j),
            )
        )
    own_v = dot(pbb[pl.ds(0, BLK), :], gbuf[...], ((1,), (0,)))

    spread_own_on(0)

    for j in (1, 2, 3):
        a_copies[1, j].wait_recv()

    def differ(p, carry):
        cols = pl.ds(pl.multiple_of(p * 2 * BLK, 2 * BLK), 2 * BLK)
        pushes = dot(vall[...], gbuf[cols, :], ((1,), (1,)))
        share = probs[:, cols]
        delta = jnp.sum(share * pushes, 0, keepdims=True)
        dsb[:, cols] = (share * (pushes - delta)).astype(jnp.bfloat16)
        return carry

    lax.fori_loop(0, GROUP // 2, differ, 0)
    for j in range(BACK, 0, -1):
        grad_k = dot(dsb[pl.ds(j * BLK, BLK), :], qbuf[...], ((1,), (0,))) * SCALE
        ksend[j - 1] = grad_k.astype(jnp.bfloat16)
        c_copies.append(
            push(
                ksend.at[j - 1], krecv.at[j - 1],
                c_send.at[1, j - 1], c_recv.at[1, j - 1], ctx(-j),
            )
        )
    own_k = dot(dsb[pl.ds(0, BLK), :], qbuf[...], ((1,), (0,))) * SCALE

    spread_other(0)
    spread_own_on(1)
    spread_other(1)

    d_copies = {}

    def collect(kind, own, received, copies, held, out_ref):
        for copy in copies:
            copy.wait_recv()
        for j in range(BACK):
            own = own + received[j].astype(jnp.float32)
        final = own.astype(jnp.bfloat16)
        held[0] = final
        out_ref[...] = final
        for r in (3, 2, 1):
            d_copies[kind, r] = push(
                held.at[0], held.at[r],
                d_send.at[kind, r - 1], d_recv.at[kind, r - 1], ctx(2 * reach[r]),
            )

    collect(0, own_v, vrecv, c_copies[:BACK], gv, ov_ref)

    def query_grads(p, carry):
        cols = pl.ds(pl.multiple_of(p * 2 * BLK, 2 * BLK), 2 * BLK)
        both = dot(dsb[:, cols], kall[...], ((0,), (0,))) * SCALE
        both = both.astype(jnp.bfloat16)
        oq_ref[:, cols] = jnp.concatenate([both[:BLK], both[BLK:]], 1)
        return carry

    lax.fori_loop(0, GROUP // 2, query_grads, 0)

    spread_other_on(0)
    spread_other_on(1)

    collect(1, own_k, krecv, c_copies[BACK:], gk, ok_ref)

    for step in (2, 3, 4, 6):
        for group in range(2):
            x2_copies[step, group].wait_recv()

    for r in range(TERMS):
        xt[:, pl.ds(r * BLK, BLK)] = xall[r].reshape(BLK, WIN).T

    e_copies = []

    def product(kind, held, acc, first, last):
        for r in range(max(first, 1), last):
            d_copies[kind, r].wait_recv()
        rows = held[first:last].reshape((last - first) * BLK, HD)
        part = dot(xt[:, first * BLK : last * BLK], rows, ((1,), (0,)))
        part = part.reshape(2, 2, 2, ROWS, HD)
        acc[...] = part if first == 0 else acc[...] + part

    def send_core(kind, acc):
        e_copies.append(
            push(
                acc.at[:, :, 1 - d], e1.at[kind],
                e_send.at[kind, 0], e_recv.at[kind, 0], core_peer,
            )
        )

    def send_others(kind, acc):
        e_copies[kind * 4].wait_recv()
        parts = ((1 - side, 1 - xl, far_peer), (1 - side, xl, side_peer), (side, 1 - xl, x_peer))
        for i, (at_side, at_x, peer) in enumerate(parts):
            both = acc[at_side, at_x, d] + e1[kind, at_side, at_x]
            u2[kind, i] = both.astype(jnp.bfloat16)
            e_copies.append(
                push(
                    u2.at[kind, i], e2.at[kind, i],
                    e_send.at[kind, i + 1], e_recv.at[kind, i + 1], peer,
                )
            )

    def total(kind, acc):
        whole = acc[side, xl, d] + e1[kind, side, xl]
        for i in range(3):
            e_copies[kind * 4 + i + 1].wait_recv()
            whole = whole + e2[kind, i].astype(jnp.float32)
        return whole

    product(0, gv, acc_v, 0, TERMS)
    send_core(0, acc_v)
    product(1, gk, acc_k, 0, TERMS - 1)
    send_others(0, acc_v)
    product(1, gk, acc_k, TERMS - 1, TERMS)
    send_core(1, acc_k)
    send_others(1, acc_k)
    ow_ref[1] = total(0, acc_v)
    ow_ref[0] = total(1, acc_k)

    for copy in list(a_copies.values()) + list(d_copies.values()) + c_copies + e_copies:
        copy.wait_send()
    for copy in [copy for _, copy in x1_copies] + list(x2_copies.values()):
        copy.wait_send()


def finish(q_ref, k_ref, v_ref, w_ref, oq_ref, ok_ref, ov_ref, ow_ref):
    oq_ref[...] = q_ref[...]
    ok_ref[...] = k_ref[...]
    ov_ref[...] = v_ref[...]
    ow_ref[:, 0, :] = w_ref[0]
    ow_ref[:, 1, :] = w_ref[1]


def local(queries, keys, values, grad_out, layer_inputs, doc_ids, member_rank, take_count):
    bf16, f32 = jnp.bfloat16, jnp.float32
    hbm = pl.BlockSpec(memory_space=pltpu.HBM)
    vmem = pl.BlockSpec(memory_space=pltpu.VMEM)
    smem = pl.BlockSpec(memory_space=pltpu.SMEM)
    dma = pltpu.SemaphoreType.DMA
    grad_q, grad_k, grad_v, grad_w = pl.pallas_call(
        kernel,
        out_shape=[
            jax.ShapeDtypeStruct((BLK, GROUP * HD), bf16),
            jax.ShapeDtypeStruct((BLK, HD), bf16),
            jax.ShapeDtypeStruct((BLK, HD), bf16),
            jax.ShapeDtypeStruct((2, ROWS, HD), f32),
        ],
        in_specs=[hbm] * 5 + [vmem, smem, smem],
        out_specs=[vmem] * 4,
        scratch_shapes=[
            pltpu.VMEM((GROUP * BLK, HD), bf16),
            pltpu.VMEM((GROUP * BLK, HD), bf16),
            pltpu.VMEM((BLK // NH, TERMS * WIN), bf16),
            pltpu.VMEM((KEYS, HD), bf16),
            pltpu.VMEM((KEYS, HD), bf16),
            pltpu.VMEM((KEYS, BLK), f32),
            pltpu.VMEM((KEYS, GROUP * BLK), f32),
            pltpu.VMEM((KEYS, GROUP * BLK), bf16),
            pltpu.VMEM((KEYS, GROUP * BLK), bf16),
            pltpu.VMEM((BACK, BLK, HD), bf16),
            pltpu.VMEM((BACK, BLK, HD), bf16),
            pltpu.VMEM((BACK, BLK, HD), bf16),
            pltpu.VMEM((BACK, BLK, HD), bf16),
            pltpu.VMEM((TERMS, NH, BLK // NH, WIN), bf16),
            pltpu.VMEM((WIN, TERMS * BLK), bf16),
            pltpu.VMEM((TERMS, BLK, HD), bf16),
            pltpu.VMEM((TERMS, BLK, HD), bf16),
            pltpu.VMEM((2, 2, 2, ROWS, HD), f32),
            pltpu.VMEM((2, 2, 2, ROWS, HD), f32),
            pltpu.VMEM((2, 2, 2, ROWS, HD), f32),
            pltpu.VMEM((2, 3, ROWS, HD), bf16),
            pltpu.VMEM((2, 3, ROWS, HD), bf16),
            dma((2 * GROUP + 3,)),
            dma((2, BACK)),
            dma((2, BACK)),
            dma((TERMS - 1,)),
            dma((TERMS - 1,)),
            dma((2, 7)),
            dma((2, 7)),
            dma((2, BACK)),
            dma((2, BACK)),
            dma((2, TERMS - 1)),
            dma((2, TERMS - 1)),
            dma((2, 4)),
            dma((2, 4)),
        ],
        compiler_params=pltpu.CompilerParams(
            collective_id=0, has_side_effects=True, vmem_limit_bytes=60 * 1024 * 1024
        ),
        cost_estimate=pl.CostEstimate(
            flops=1300000000, bytes_accessed=2000000, transcendentals=700000
        ),
    )(
        queries[0], keys[0], values[0], grad_out[0], layer_inputs[0],
        doc_ids, member_rank, take_count,
    )
    grad_q, grad_k, grad_v, grad_w = pl.pallas_call(
        finish,
        out_shape=[
            jax.ShapeDtypeStruct((BLK, GROUP * HD), bf16),
            jax.ShapeDtypeStruct((BLK, HD), bf16),
            jax.ShapeDtypeStruct((BLK, HD), bf16),
            jax.ShapeDtypeStruct((ROWS, 2, HD), f32),
        ],
        in_specs=[vmem] * 4,
        out_specs=[vmem] * 4,
    )(grad_q, grad_k, grad_v, grad_w)
    return (grad_q[None], grad_k[None], grad_v[None], grad_w)


def solution(mesh):
    in_specs = (
        P("dp", "ctx", "head"),
        P("dp", "ctx", "head"),
        P("dp", "ctx", "head"),
        P("dp", "ctx", "head"),
        P("dp", ("ctx", "head"), None),
        P("dp", None),
        P(),
        P(),
    )
    out_specs = (
        P("dp", "ctx", "head"),
        P("dp", "ctx", "head"),
        P("dp", "ctx", "head"),
        P(("ctx", "dp"), None, "head"),
    )
    return jax.shard_map(local, mesh=mesh, in_specs=in_specs, out_specs=out_specs, check_vma=False)
```

```python
import math

import jax
import jax.numpy as jnp
from jax import lax
from jax.experimental import pallas as pl
from jax.experimental.pallas import tpu as pltpu
from jax.sharding import PartitionSpec as P

HD = 128
BLK = 128
NCTX = 16
NZ = 8
NY = 4
NH = 8
GROUP = 8
WIN = 1280
ROWS = 160
BACK = 4
KEYS = (BACK + 1) * BLK
NEG = -1e30
TERMS = 4
SCALE = 1.0 / math.sqrt(HD)
MESH = pl.DeviceIdType.MESH


def dot(a, b, dims):
    return lax.dot_general(a, b, (dims, ((), ())), preferred_element_type=jnp.float32)


def kernel(
    q_hbm, k_hbm, v_hbm, g_hbm, x_hbm, doc_ref, rank_ref, take_ref,
    oq_ref, ok_ref, ov_ref, ow_ref,
    qbuf, gbuf, xbuf, kall, vall, bias, probs, dsb, pbb, vsend, vrecv, ksend, krecv,
    xall, xt, gv, gk, acc_v, acc_k, e1, u2, e2,
    loc_sem, a_send, a_recv, x1_send, x1_recv, x2_send, x2_recv,
    c_send, c_recv, d_send, d_recv, e_send, e_recv,
):
    c = lax.axis_index("ctx")
    h = lax.axis_index("head")
    d = lax.axis_index("dp")
    z, xl = c // 2, c % 2
    xh, y = h // NY, h % NY
    side = z % 2
    way = 1 - 2 * side

    def ctx(delta):
        return {"ctx": (c + delta + NCTX) % NCTX}

    def head_index(dx, dy):
        return ((xh + dx) % 2) * NY + (y + dy + NY) % NY

    def head(dx, dy):
        return {"head": head_index(dx, dy)}

    core_peer = {"dp": 1 - d}
    side_peer = {"ctx": c + 2 * way}
    x_peer = {"ctx": c + 1 - 2 * xl}
    far_peer = {"ctx": c + 2 * way + 1 - 2 * xl}
    reach = {1: -way, 2: 2 * way, 3: -3 * way}

    barrier = pltpu.get_barrier_semaphore()
    peers = [ctx(s) for s in (1, 2, 3, 4, -1, -2, -3, -4)] + [ctx(-6 * way)]
    peers += [head(1, 0), head(0, 1), head(0, 2), head(0, 3), core_peer]
    for peer in peers:
        pl.semaphore_signal(barrier, inc=1, device_id=peer, device_id_type=MESH)

    local = []

    def fetch(src, dst):
        copy = pltpu.make_async_copy(src, dst, loc_sem.at[len(local)])
        copy.start()
        local.append(copy)

    fetch(k_hbm, kall.at[pl.ds(0, BLK)])
    fetch(v_hbm, vall.at[pl.ds(0, BLK)])
    fetch(x_hbm, xbuf)
    for n in range(GROUP):
        fetch(q_hbm.at[:, pl.ds(n * HD, HD)], qbuf.at[pl.ds(n * BLK, BLK)])
        fetch(g_hbm.at[:, pl.ds(n * HD, HD)], gbuf.at[pl.ds(n * BLK, BLK)])

    down = lax.broadcasted_iota(jnp.int32, (BLK, BLK), 0)
    across = lax.broadcasted_iota(jnp.int32, (BLK, BLK), 1)
    excluded = jnp.int32(0)
    end = jnp.int32(0)
    count_down = jnp.zeros((BLK, BLK), jnp.int32)
    count_across = jnp.zeros((BLK, BLK), jnp.int32)
    for b in range(NCTX):
        excluded = excluded + jnp.where(rank_ref[b] < 0, b, 0)
        end = end + take_ref[b]
        count_down = count_down + jnp.where(down >= end, 1, 0)
        count_across = count_across + jnp.where(across >= end, 1, 0)
    taken_down = count_down - jnp.where(count_down > excluded, 1, 0)
    taken_across = count_across - jnp.where(count_across > excluded, 1, 0)
    my_rank = jnp.full((BLK, BLK), rank_ref[c], jnp.int32)
    slot_t = jnp.where(my_rank < 0, taken_across, my_rank)
    doc_t = jnp.broadcast_to(
        doc_ref[:, pl.ds(pl.multiple_of(c * BLK, BLK), BLK)], (BLK, BLK)
    )
    for j in range(BACK + 1):
        b = (c - j + NCTX) % NCTX
        rank = jnp.full((BLK, BLK), rank_ref[b], jnp.int32)
        gap = slot_t - jnp.where(rank < 0, taken_down, rank)
        doc_u = jnp.broadcast_to(
            doc_ref[:, pl.ds(pl.multiple_of(b * BLK, BLK), BLK)], (BLK, BLK)
        ).T
        order = (c * BLK + across) - (b * BLK + down)
        seen = (doc_u == doc_t) & (order >= 0) & (gap >= 0) & (gap <= 2)
        bias[pl.ds(j * BLK, BLK), :] = jnp.where(seen, 0.0, NEG)

    for copy in local:
        copy.wait()
    xall[0, h] = xbuf[:, pl.ds(pl.multiple_of((z // 2) * WIN, 128), WIN)]
    pl.semaphore_wait(barrier, len(peers))

    def push(src, dst, send, recv, peer):
        copy = pltpu.make_async_remote_copy(
            src_ref=src, dst_ref=dst, send_sem=send, recv_sem=recv,
            device_id=peer, device_id_type=MESH,
        )
        copy.start()
        return copy

    a_copies = {}

    def hand_on(kind, held, j, source, peer):
        a_copies[kind, j] = push(
            held.at[pl.ds(source, BLK)], held.at[pl.ds(j * BLK, BLK)],
            a_send.at[kind, j - 1], a_recv.at[kind, j - 1], peer,
        )

    hand_on(0, kall, 4, 0, ctx(4))
    hand_on(1, vall, 4, 0, ctx(4))
    hand_on(0, kall, 2, 0, ctx(2))
    hand_on(0, kall, 1, 0, ctx(1))
    x1_copies = []
    for r in (3, 2, 1):
        there = (z + reach[r] + NZ) % NZ // 2
        copy = push(
            xbuf.at[:, pl.ds(pl.multiple_of(there * WIN, 128), WIN)],
            xall.at[r, h], x1_send.at[r - 1], x1_recv.at[r - 1], ctx(2 * reach[r]),
        )
        x1_copies.append((r, copy))
    hand_on(1, vall, 2, 0, ctx(2))
    hand_on(1, vall, 1, 0, ctx(1))
    third = pl.multiple_of(xl * BACK * BLK, BLK)
    third_peer = {"ctx": (c + 3 - 4 * xl + NCTX) % NCTX}
    for kind, held in ((0, kall), (1, vall)):
        a_copies[kind, 4].wait_recv()
        hand_on(kind, held, 3, third, third_peer)
    x2_copies = {}

    def spread(step, group, at, peer):
        part = xall.at[pl.ds(2 * group, 2), at]
        x2_copies[step, group] = push(
            part, part, x2_send.at[group, step], x2_recv.at[group, step], peer
        )

    def spread_own(group):
        for copy in x1_copies:
            if copy[0] // 2 == group:
                copy[1].wait_recv()
        spread(0, group, h, head(1, 0))
        spread(1, group, h, head(0, 1))
        spread(2, group, h, head(0, -1))

    def spread_own_on(group):
        x2_copies[1, group].wait_recv()
        spread(3, group, head_index(0, -1), head(0, 1))

    def spread_other(group):
        x2_copies[0, group].wait_recv()
        spread(4, group, head_index(1, 0), head(0, 1))
        spread(5, group, head_index(1, 0), head(0, -1))

    def spread_other_on(group):
        x2_copies[5, group].wait_recv()
        spread(6, group, head_index(1, 1), head(0, -1))

    spread_own(0)
    spread_own(1)
    for j in (1, 2, 3):
        a_copies[0, j].wait_recv()

    def weigh(p, carry):
        cols = pl.ds(pl.multiple_of(p * 2 * BLK, 2 * BLK), 2 * BLK)
        hidden = bias[...]
        scores = dot(kall[...], qbuf[cols, :], ((1,), (1,))) * SCALE
        scores = scores + jnp.concatenate([hidden, hidden], 1)
        top = jnp.max(scores, 0, keepdims=True)
        weights = jnp.exp(scores - top)
        total = jnp.sum(weights, 0, keepdims=True)
        share = weights * (1.0 / total)
        probs[:, cols] = share
        pbb[:, cols] = share.astype(jnp.bfloat16)
        return carry

    lax.fori_loop(0, GROUP // 2, weigh, 0)
    c_copies = []
    for j in range(BACK, 0, -1):
        grad_v = dot(pbb[pl.ds(j * BLK, BLK), :], gbuf[...], ((1,), (0,)))
        vsend[j - 1] = grad_v.astype(jnp.bfloat16)
        c_copies.append(
            push(
                vsend.at[j - 1], vrecv.at[j - 1],
                c_send.at[0, j - 1], c_recv.at[0, j - 1], ctx(-j),
            )
        )
    own_v = dot(pbb[pl.ds(0, BLK), :], gbuf[...], ((1,), (0,)))

    spread_own_on(0)

    for j in (1, 2, 3):
        a_copies[1, j].wait_recv()

    def differ(p, carry):
        cols = pl.ds(pl.multiple_of(p * 2 * BLK, 2 * BLK), 2 * BLK)
        pushes = dot(vall[...], gbuf[cols, :], ((1,), (1,)))
        share = probs[:, cols]
        delta = jnp.sum(share * pushes, 0, keepdims=True)
        dsb[:, cols] = (share * (pushes - delta)).astype(jnp.bfloat16)
        return carry

    lax.fori_loop(0, GROUP // 2, differ, 0)
    for j in range(BACK, 0, -1):
        grad_k = dot(dsb[pl.ds(j * BLK, BLK), :], qbuf[...], ((1,), (0,))) * SCALE
        ksend[j - 1] = grad_k.astype(jnp.bfloat16)
        c_copies.append(
            push(
                ksend.at[j - 1], krecv.at[j - 1],
                c_send.at[1, j - 1], c_recv.at[1, j - 1], ctx(-j),
            )
        )
    own_k = dot(dsb[pl.ds(0, BLK), :], qbuf[...], ((1,), (0,))) * SCALE

    spread_other(0)
    spread_own_on(1)
    spread_other(1)

    d_copies = {}

    def collect(kind, own, received, copies, held, out_ref):
        for copy in copies:
            copy.wait_recv()
        for j in range(BACK):
            own = own + received[j].astype(jnp.float32)
        final = own.astype(jnp.bfloat16)
        held[0] = final
        out_ref[...] = final
        for r in (3, 2, 1):
            d_copies[kind, r] = push(
                held.at[0], held.at[r],
                d_send.at[kind, r - 1], d_recv.at[kind, r - 1], ctx(2 * reach[r]),
            )

    collect(0, own_v, vrecv, c_copies[:BACK], gv, ov_ref)

    def query_grads(p, carry):
        cols = pl.ds(pl.multiple_of(p * 2 * BLK, 2 * BLK), 2 * BLK)
        both = dot(dsb[:, cols], kall[...], ((0,), (0,))) * SCALE
        both = both.astype(jnp.bfloat16)
        oq_ref[:, cols] = jnp.concatenate([both[:BLK], both[BLK:]], 1)
        return carry

    lax.fori_loop(0, GROUP // 2, query_grads, 0)

    spread_other_on(0)
    spread_other_on(1)

    collect(1, own_k, krecv, c_copies[BACK:], gk, ok_ref)

    for step in (2, 3, 4, 6):
        for group in range(2):
            x2_copies[step, group].wait_recv()

    for r in range(TERMS):
        xt[:, pl.ds(r * BLK, BLK)] = xall[r].reshape(BLK, WIN).T

    e_copies = []

    def product(kind, held, acc, first, last):
        for r in range(max(first, 1), last):
            d_copies[kind, r].wait_recv()
        rows = held[first:last].reshape((last - first) * BLK, HD)
        part = dot(xt[:, first * BLK : last * BLK], rows, ((1,), (0,)))
        part = part.reshape(2, 2, 2, ROWS, HD)
        acc[...] = part if first == 0 else acc[...] + part

    def send_core(kind, acc):
        e_copies.append(
            push(
                acc.at[:, :, 1 - d], e1.at[kind],
                e_send.at[kind, 0], e_recv.at[kind, 0], core_peer,
            )
        )

    def send_others(kind, acc):
        e_copies[kind * 4].wait_recv()
        parts = ((1 - side, 1 - xl, far_peer), (1 - side, xl, side_peer), (side, 1 - xl, x_peer))
        for i, (at_side, at_x, peer) in enumerate(parts):
            both = acc[at_side, at_x, d] + e1[kind, at_side, at_x]
            u2[kind, i] = both.astype(jnp.bfloat16)
            e_copies.append(
                push(
                    u2.at[kind, i], e2.at[kind, i],
                    e_send.at[kind, i + 1], e_recv.at[kind, i + 1], peer,
                )
            )

    def total(kind, acc):
        whole = acc[side, xl, d] + e1[kind, side, xl]
        for i in range(3):
            e_copies[kind * 4 + i + 1].wait_recv()
            whole = whole + e2[kind, i].astype(jnp.float32)
        return whole

    product(0, gv, acc_v, 0, TERMS)
    send_core(0, acc_v)
    product(1, gk, acc_k, 0, TERMS - 1)
    send_others(0, acc_v)
    product(1, gk, acc_k, TERMS - 1, TERMS)
    send_core(1, acc_k)
    send_others(1, acc_k)
    ow_ref[1] = total(0, acc_v)
    ow_ref[0] = total(1, acc_k)

    for copy in list(a_copies.values()) + list(d_copies.values()) + c_copies + e_copies:
        copy.wait_send()
    for copy in [copy for _, copy in x1_copies] + list(x2_copies.values()):
        copy.wait_send()


def finish(q_ref, k_ref, v_ref, w_ref, oq_ref, ok_ref, ov_ref, ow_ref):
    oq_ref[...] = q_ref[...]
    ok_ref[...] = k_ref[...]
    ov_ref[...] = v_ref[...]
    ow_ref[:, 0, :] = w_ref[0]
    ow_ref[:, 1, :] = w_ref[1]


def local(queries, keys, values, grad_out, layer_inputs, doc_ids, member_rank, take_count):
    bf16, f32 = jnp.bfloat16, jnp.float32
    hbm = pl.BlockSpec(memory_space=pltpu.HBM)
    vmem = pl.BlockSpec(memory_space=pltpu.VMEM)
    smem = pl.BlockSpec(memory_space=pltpu.SMEM)
    dma = pltpu.SemaphoreType.DMA
    grad_q, grad_k, grad_v, grad_w = pl.pallas_call(
        kernel,
        out_shape=[
            pltpu.VMEM((BLK, GROUP * HD), bf16),
            pltpu.VMEM((BLK, HD), bf16),
            pltpu.VMEM((BLK, HD), bf16),
            pltpu.VMEM((2, ROWS, HD), f32),
        ],
        in_specs=[hbm] * 5 + [vmem, smem, smem],
        out_specs=[vmem] * 4,
        scratch_shapes=[
            pltpu.VMEM((GROUP * BLK, HD), bf16),
            pltpu.VMEM((GROUP * BLK, HD), bf16),
            pltpu.VMEM((BLK // NH, TERMS * WIN), bf16),
            pltpu.VMEM((KEYS, HD), bf16),
            pltpu.VMEM((KEYS, HD), bf16),
            pltpu.VMEM((KEYS, BLK), f32),
            pltpu.VMEM((KEYS, GROUP * BLK), f32),
            pltpu.VMEM((KEYS, GROUP * BLK), bf16),
            pltpu.VMEM((KEYS, GROUP * BLK), bf16),
            pltpu.VMEM((BACK, BLK, HD), bf16),
            pltpu.VMEM((BACK, BLK, HD), bf16),
            pltpu.VMEM((BACK, BLK, HD), bf16),
            pltpu.VMEM((BACK, BLK, HD), bf16),
            pltpu.VMEM((TERMS, NH, BLK // NH, WIN), bf16),
            pltpu.VMEM((WIN, TERMS * BLK), bf16),
            pltpu.VMEM((TERMS, BLK, HD), bf16),
            pltpu.VMEM((TERMS, BLK, HD), bf16),
            pltpu.VMEM((2, 2, 2, ROWS, HD), f32),
            pltpu.VMEM((2, 2, 2, ROWS, HD), f32),
            pltpu.VMEM((2, 2, 2, ROWS, HD), f32),
            pltpu.VMEM((2, 3, ROWS, HD), bf16),
            pltpu.VMEM((2, 3, ROWS, HD), bf16),
            dma((2 * GROUP + 3,)),
            dma((2, BACK)),
            dma((2, BACK)),
            dma((TERMS - 1,)),
            dma((TERMS - 1,)),
            dma((2, 7)),
            dma((2, 7)),
            dma((2, BACK)),
            dma((2, BACK)),
            dma((2, TERMS - 1)),
            dma((2, TERMS - 1)),
            dma((2, 4)),
            dma((2, 4)),
        ],
        compiler_params=pltpu.CompilerParams(
            collective_id=0, has_side_effects=True, vmem_limit_bytes=60 * 1024 * 1024
        ),
        cost_estimate=pl.CostEstimate(
            flops=1300000000, bytes_accessed=2000000, transcendentals=700000
        ),
    )(
        queries[0], keys[0], values[0], grad_out[0], layer_inputs[0],
        doc_ids, member_rank, take_count,
    )
    grad_q, grad_k, grad_v, grad_w = pl.pallas_call(
        finish,
        out_shape=[
            jax.ShapeDtypeStruct((BLK, GROUP * HD), bf16),
            jax.ShapeDtypeStruct((BLK, HD), bf16),
            jax.ShapeDtypeStruct((BLK, HD), bf16),
            jax.ShapeDtypeStruct((ROWS, 2, HD), f32),
        ],
        in_specs=[vmem] * 4,
        out_specs=[vmem] * 4,
        compiler_params=pltpu.CompilerParams(vmem_limit_bytes=4 * 1024 * 1024),
    )(grad_q, grad_k, grad_v, grad_w)
    return (grad_q[None], grad_k[None], grad_v[None], grad_w)


def solution(mesh):
    in_specs = (
        P("dp", "ctx", "head"),
        P("dp", "ctx", "head"),
        P("dp", "ctx", "head"),
        P("dp", "ctx", "head"),
        P("dp", ("ctx", "head"), None),
        P("dp", None),
        P(),
        P(),
    )
    out_specs = (
        P("dp", "ctx", "head"),
        P("dp", "ctx", "head"),
        P("dp", "ctx", "head"),
        P(("ctx", "dp"), None, "head"),
    )
    return jax.shard_map(local, mesh=mesh, in_specs=in_specs, out_specs=out_specs, check_vma=False)
```

```python
import math

import jax
import jax.numpy as jnp
from jax import lax
from jax.experimental import pallas as pl
from jax.experimental.pallas import tpu as pltpu
from jax.sharding import PartitionSpec as P

HD = 128
BLK = 128
NCTX = 16
NZ = 8
NY = 4
NH = 8
GROUP = 8
WIN = 1280
ROWS = 160
BACK = 4
KEYS = (BACK + 1) * BLK
NEG = -1e30
TERMS = 4
SCALE = 1.0 / math.sqrt(HD)
MESH = pl.DeviceIdType.MESH


def dot(a, b, dims):
    return lax.dot_general(a, b, (dims, ((), ())), preferred_element_type=jnp.float32)


def kernel(
    q_hbm, k_hbm, v_hbm, g_hbm, x_hbm, doc_ref, rank_ref, take_ref,
    oq_ref, ok_ref, ov_ref, ow_ref,
    qbuf, gbuf, xbuf, kall, vall, bias, probs, pushes, dsb, pbb, vsend, vrecv, ksend, krecv,
    xall, xt, gv, gk, acc_v, acc_k, e1, u2, e2,
    loc_sem, a_send, a_recv, x1_send, x1_recv, x2_send, x2_recv,
    c_send, c_recv, d_send, d_recv, e_send, e_recv,
):
    c = lax.axis_index("ctx")
    h = lax.axis_index("head")
    d = lax.axis_index("dp")
    z, xl = c // 2, c % 2
    xh, y = h // NY, h % NY
    side = z % 2
    way = 1 - 2 * side

    def ctx(delta):
        return {"ctx": (c + delta + NCTX) % NCTX}

    def head_index(dx, dy):
        return ((xh + dx) % 2) * NY + (y + dy + NY) % NY

    def head(dx, dy):
        return {"head": head_index(dx, dy)}

    core_peer = {"dp": 1 - d}
    side_peer = {"ctx": c + 2 * way}
    x_peer = {"ctx": c + 1 - 2 * xl}
    far_peer = {"ctx": c + 2 * way + 1 - 2 * xl}
    reach = {1: -way, 2: 2 * way, 3: -3 * way}

    barrier = pltpu.get_barrier_semaphore()
    peers = [ctx(s) for s in (1, 2, 3, 4, -1, -2, -3, -4)] + [ctx(-6 * way)]
    peers += [head(1, 0), head(0, 1), head(0, 2), head(0, 3), core_peer]
    for peer in peers:
        pl.semaphore_signal(barrier, inc=1, device_id=peer, device_id_type=MESH)

    local = []

    def fetch(src, dst):
        copy = pltpu.make_async_copy(src, dst, loc_sem.at[len(local)])
        copy.start()
        local.append(copy)

    fetch(k_hbm, kall.at[pl.ds(0, BLK)])
    fetch(v_hbm, vall.at[pl.ds(0, BLK)])
    fetch(x_hbm, xbuf)
    for n in range(GROUP):
        fetch(q_hbm.at[:, pl.ds(n * HD, HD)], qbuf.at[pl.ds(n * BLK, BLK)])
        fetch(g_hbm.at[:, pl.ds(n * HD, HD)], gbuf.at[pl.ds(n * BLK, BLK)])

    down = lax.broadcasted_iota(jnp.int32, (BLK, BLK), 0)
    across = lax.broadcasted_iota(jnp.int32, (BLK, BLK), 1)
    excluded = jnp.int32(0)
    end = jnp.int32(0)
    count_down = jnp.zeros((BLK, BLK), jnp.int32)
    count_across = jnp.zeros((BLK, BLK), jnp.int32)
    for b in range(NCTX):
        excluded = excluded + jnp.where(rank_ref[b] < 0, b, 0)
        end = end + take_ref[b]
        count_down = count_down + jnp.where(down >= end, 1, 0)
        count_across = count_across + jnp.where(across >= end, 1, 0)
    taken_down = count_down - jnp.where(count_down > excluded, 1, 0)
    taken_across = count_across - jnp.where(count_across > excluded, 1, 0)
    my_rank = jnp.full((BLK, BLK), rank_ref[c], jnp.int32)
    slot_t = jnp.where(my_rank < 0, taken_across, my_rank)
    doc_t = jnp.broadcast_to(
        doc_ref[:, pl.ds(pl.multiple_of(c * BLK, BLK), BLK)], (BLK, BLK)
    )
    for j in range(BACK + 1):
        b = (c - j + NCTX) % NCTX
        rank = jnp.full((BLK, BLK), rank_ref[b], jnp.int32)
        gap = slot_t - jnp.where(rank < 0, taken_down, rank)
        doc_u = jnp.broadcast_to(
            doc_ref[:, pl.ds(pl.multiple_of(b * BLK, BLK), BLK)], (BLK, BLK)
        ).T
        order = (c * BLK + across) - (b * BLK + down)
        seen = (doc_u == doc_t) & (order >= 0) & (gap >= 0) & (gap <= 2)
        bias[pl.ds(j * BLK, BLK), :] = jnp.where(seen, 0.0, NEG)

    for copy in local:
        copy.wait()
    xall[0, h] = xbuf[:, pl.ds(pl.multiple_of((z // 2) * WIN, 128), WIN)]

    chunks = [pl.ds(p * 2 * BLK, 2 * BLK) for p in range(GROUP // 2)]
    tops = [jnp.full((1, 2 * BLK), NEG, jnp.float32) for _ in chunks]

    def score(first, last):
        rows = pl.ds(first * BLK, (last - first) * BLK)
        hidden = bias[rows, :]
        hidden = jnp.concatenate([hidden, hidden], 1)
        for p, cols in enumerate(chunks):
            part = dot(kall[rows, :], qbuf[cols, :], ((1,), (1,))) * SCALE + hidden
            probs[rows, cols] = part
            tops[p] = jnp.maximum(tops[p], jnp.max(part, 0, keepdims=True))

    def value_products(first, last):
        rows = pl.ds(first * BLK, (last - first) * BLK)
        for cols in chunks:
            pushes[rows, cols] = dot(vall[rows, :], gbuf[cols, :], ((1,), (1,)))

    score(0, 1)
    value_products(0, 1)
    pl.semaphore_wait(barrier, len(peers))

    def push(src, dst, send, recv, peer):
        copy = pltpu.make_async_remote_copy(
            src_ref=src, dst_ref=dst, send_sem=send, recv_sem=recv,
            device_id=peer, device_id_type=MESH,
        )
        copy.start()
        return copy

    a_copies = {}

    def hand_on(kind, held, j, source, peer):
        a_copies[kind, j] = push(
            held.at[pl.ds(source, BLK)], held.at[pl.ds(j * BLK, BLK)],
            a_send.at[kind, j - 1], a_recv.at[kind, j - 1], peer,
        )

    hand_on(0, kall, 4, 0, ctx(4))
    hand_on(1, vall, 4, 0, ctx(4))
    hand_on(0, kall, 2, 0, ctx(2))
    hand_on(0, kall, 1, 0, ctx(1))
    x1_copies = []
    for r in (3, 2, 1):
        there = (z + reach[r] + NZ) % NZ // 2
        copy = push(
            xbuf.at[:, pl.ds(pl.multiple_of(there * WIN, 128), WIN)],
            xall.at[r, h], x1_send.at[r - 1], x1_recv.at[r - 1], ctx(2 * reach[r]),
        )
        x1_copies.append((r, copy))
    hand_on(1, vall, 2, 0, ctx(2))
    hand_on(1, vall, 1, 0, ctx(1))
    third = pl.multiple_of(xl * BACK * BLK, BLK)
    third_peer = {"ctx": (c + 3 - 4 * xl + NCTX) % NCTX}
    for kind, held in ((0, kall), (1, vall)):
        a_copies[kind, 4].wait_recv()
        hand_on(kind, held, 3, third, third_peer)
    score(4, 5)
    value_products(4, 5)
    x2_copies = {}

    def spread(step, group, at, peer):
        part = xall.at[pl.ds(2 * group, 2), at]
        x2_copies[step, group] = push(
            part, part, x2_send.at[group, step], x2_recv.at[group, step], peer
        )

    def spread_own(group):
        for copy in x1_copies:
            if copy[0] // 2 == group:
                copy[1].wait_recv()
        spread(0, group, h, head(1, 0))
        spread(1, group, h, head(0, 1))
        spread(2, group, h, head(0, -1))

    def spread_own_on(group):
        x2_copies[1, group].wait_recv()
        spread(3, group, head_index(0, -1), head(0, 1))

    def spread_other(group):
        x2_copies[0, group].wait_recv()
        spread(4, group, head_index(1, 0), head(0, 1))
        spread(5, group, head_index(1, 0), head(0, -1))

    def spread_other_on(group):
        x2_copies[5, group].wait_recv()
        spread(6, group, head_index(1, 1), head(0, -1))

    spread_own(0)
    spread_own(1)
    for j in (1, 2):
        a_copies[0, j].wait_recv()
    score(1, 3)
    a_copies[0, 3].wait_recv()
    score(3, 4)

    inverse = []
    for p, cols in enumerate(chunks):
        weights = jnp.exp(probs[:, cols] - tops[p])
        probs[:, cols] = weights
        inverse.append(1.0 / jnp.sum(weights, 0, keepdims=True))
    inverse = jnp.concatenate(inverse, 1)
    c_copies = []

    def send_back(kind, j, held, received, grad):
        held[j - 1] = grad.astype(jnp.bfloat16)
        c_copies.append(
            push(
                held.at[j - 1], received.at[j - 1],
                c_send.at[kind, j - 1], c_recv.at[kind, j - 1], ctx(-j),
            )
        )

    for j in range(BACK, -1, -1):
        rows = pl.ds(j * BLK, BLK)
        share = probs[rows, :] * inverse
        probs[rows, :] = share
        pbb[rows, :] = share.astype(jnp.bfloat16)
        own_v = dot(pbb[rows, :], gbuf[...], ((1,), (0,)))
        if j > 0:
            send_back(0, j, vsend, vrecv, own_v)

    spread_own_on(0)

    for j in (1, 2):
        a_copies[1, j].wait_recv()
    value_products(1, 3)
    a_copies[1, 3].wait_recv()
    value_products(3, 4)
    delta = [
        jnp.sum(probs[:, cols] * pushes[:, cols], 0, keepdims=True) for cols in chunks
    ]
    delta = jnp.concatenate(delta, 1)
    for j in range(BACK, -1, -1):
        rows = pl.ds(j * BLK, BLK)
        change = probs[rows, :] * (pushes[rows, :] - delta)
        dsb[rows, :] = change.astype(jnp.bfloat16)
        own_k = dot(dsb[rows, :], qbuf[...], ((1,), (0,))) * SCALE
        if j > 0:
            send_back(1, j, ksend, krecv, own_k)

    spread_other(0)
    spread_own_on(1)
    spread_other(1)

    d_copies = {}

    def collect(kind, own, received, copies, held, out_ref):
        for copy in copies:
            copy.wait_recv()
        for j in range(BACK):
            own = own + received[j].astype(jnp.float32)
        final = own.astype(jnp.bfloat16)
        held[0] = final
        out_ref[...] = final
        for r in (3, 2, 1):
            d_copies[kind, r] = push(
                held.at[0], held.at[r],
                d_send.at[kind, r - 1], d_recv.at[kind, r - 1], ctx(2 * reach[r]),
            )

    collect(0, own_v, vrecv, c_copies[:BACK], gv, ov_ref)

    def query_grads(p, carry):
        cols = pl.ds(pl.multiple_of(p * 2 * BLK, 2 * BLK), 2 * BLK)
        both = dot(dsb[:, cols], kall[...], ((0,), (0,))) * SCALE
        both = both.astype(jnp.bfloat16)
        oq_ref[:, cols] = jnp.concatenate([both[:BLK], both[BLK:]], 1)
        return carry

    lax.fori_loop(0, GROUP // 2, query_grads, 0)

    spread_other_on(0)
    spread_other_on(1)

    collect(1, own_k, krecv, c_copies[BACK:], gk, ok_ref)

    for step in (2, 3, 4, 6):
        for group in range(2):
            x2_copies[step, group].wait_recv()

    for r in range(TERMS):
        xt[:, pl.ds(r * BLK, BLK)] = xall[r].reshape(BLK, WIN).T

    e_copies = []

    def product(kind, held, acc, first, last):
        for r in range(max(first, 1), last):
            d_copies[kind, r].wait_recv()
        rows = held[first:last].reshape((last - first) * BLK, HD)
        part = dot(xt[:, first * BLK : last * BLK], rows, ((1,), (0,)))
        part = part.reshape(2, 2, 2, ROWS, HD)
        acc[...] = part if first == 0 else acc[...] + part

    def send_core(kind, acc):
        e_copies.append(
            push(
                acc.at[:, :, 1 - d], e1.at[kind],
                e_send.at[kind, 0], e_recv.at[kind, 0], core_peer,
            )
        )

    def send_others(kind, acc):
        e_copies[kind * 4].wait_recv()
        parts = ((1 - side, 1 - xl, far_peer), (1 - side, xl, side_peer), (side, 1 - xl, x_peer))
        for i, (at_side, at_x, peer) in enumerate(parts):
            both = acc[at_side, at_x, d] + e1[kind, at_side, at_x]
            u2[kind, i] = both.astype(jnp.bfloat16)
            e_copies.append(
                push(
                    u2.at[kind, i], e2.at[kind, i],
                    e_send.at[kind, i + 1], e_recv.at[kind, i + 1], peer,
                )
            )

    def total(kind, acc):
        whole = acc[side, xl, d] + e1[kind, side, xl]
        for i in range(3):
            e_copies[kind * 4 + i + 1].wait_recv()
            whole = whole + e2[kind, i].astype(jnp.float32)
        return whole

    product(0, gv, acc_v, 0, TERMS)
    send_core(0, acc_v)
    product(1, gk, acc_k, 0, TERMS - 1)
    send_others(0, acc_v)
    product(1, gk, acc_k, TERMS - 1, TERMS)
    send_core(1, acc_k)
    send_others(1, acc_k)
    ow_ref[1] = total(0, acc_v)
    ow_ref[0] = total(1, acc_k)

    for copy in list(a_copies.values()) + list(d_copies.values()) + c_copies + e_copies:
        copy.wait_send()
    for copy in [copy for _, copy in x1_copies] + list(x2_copies.values()):
        copy.wait_send()


def finish(q_ref, k_ref, v_ref, w_ref, oq_ref, ok_ref, ov_ref, ow_ref):
    oq_ref[...] = q_ref[...]
    ok_ref[...] = k_ref[...]
    ov_ref[...] = v_ref[...]
    ow_ref[:, 0, :] = w_ref[0]
    ow_ref[:, 1, :] = w_ref[1]


def local(queries, keys, values, grad_out, layer_inputs, doc_ids, member_rank, take_count):
    bf16, f32 = jnp.bfloat16, jnp.float32
    hbm = pl.BlockSpec(memory_space=pltpu.HBM)
    vmem = pl.BlockSpec(memory_space=pltpu.VMEM)
    smem = pl.BlockSpec(memory_space=pltpu.SMEM)
    dma = pltpu.SemaphoreType.DMA
    grad_q, grad_k, grad_v, grad_w = pl.pallas_call(
        kernel,
        out_shape=[
            pltpu.VMEM((BLK, GROUP * HD), bf16),
            pltpu.VMEM((BLK, HD), bf16),
            pltpu.VMEM((BLK, HD), bf16),
            pltpu.VMEM((2, ROWS, HD), f32),
        ],
        in_specs=[hbm] * 5 + [vmem, smem, smem],
        out_specs=[vmem] * 4,
        scratch_shapes=[
            pltpu.VMEM((GROUP * BLK, HD), bf16),
            pltpu.VMEM((GROUP * BLK, HD), bf16),
            pltpu.VMEM((BLK // NH, TERMS * WIN), bf16),
            pltpu.VMEM((KEYS, HD), bf16),
            pltpu.VMEM((KEYS, HD), bf16),
            pltpu.VMEM((KEYS, BLK), f32),
            pltpu.VMEM((KEYS, GROUP * BLK), f32),
            pltpu.VMEM((KEYS, GROUP * BLK), f32),
            pltpu.VMEM((KEYS, GROUP * BLK), bf16),
            pltpu.VMEM((KEYS, GROUP * BLK), bf16),
            pltpu.VMEM((BACK, BLK, HD), bf16),
            pltpu.VMEM((BACK, BLK, HD), bf16),
            pltpu.VMEM((BACK, BLK, HD), bf16),
            pltpu.VMEM((BACK, BLK, HD), bf16),
            pltpu.VMEM((TERMS, NH, BLK // NH, WIN), bf16),
            pltpu.VMEM((WIN, TERMS * BLK), bf16),
            pltpu.VMEM((TERMS, BLK, HD), bf16),
            pltpu.VMEM((TERMS, BLK, HD), bf16),
            pltpu.VMEM((2, 2, 2, ROWS, HD), f32),
            pltpu.VMEM((2, 2, 2, ROWS, HD), f32),
            pltpu.VMEM((2, 2, 2, ROWS, HD), f32),
            pltpu.VMEM((2, 3, ROWS, HD), bf16),
            pltpu.VMEM((2, 3, ROWS, HD), bf16),
            dma((2 * GROUP + 3,)),
            dma((2, BACK)),
            dma((2, BACK)),
            dma((TERMS - 1,)),
            dma((TERMS - 1,)),
            dma((2, 7)),
            dma((2, 7)),
            dma((2, BACK)),
            dma((2, BACK)),
            dma((2, TERMS - 1)),
            dma((2, TERMS - 1)),
            dma((2, 4)),
            dma((2, 4)),
        ],
        compiler_params=pltpu.CompilerParams(
            collective_id=0, has_side_effects=True, vmem_limit_bytes=60 * 1024 * 1024
        ),
        cost_estimate=pl.CostEstimate(
            flops=1300000000, bytes_accessed=2000000, transcendentals=700000
        ),
    )(
        queries[0], keys[0], values[0], grad_out[0], layer_inputs[0],
        doc_ids, member_rank, take_count,
    )
    grad_q, grad_k, grad_v, grad_w = pl.pallas_call(
        finish,
        out_shape=[
            jax.ShapeDtypeStruct((BLK, GROUP * HD), bf16),
            jax.ShapeDtypeStruct((BLK, HD), bf16),
            jax.ShapeDtypeStruct((BLK, HD), bf16),
            jax.ShapeDtypeStruct((ROWS, 2, HD), f32),
        ],
        in_specs=[vmem] * 4,
        out_specs=[vmem] * 4,
        compiler_params=pltpu.CompilerParams(vmem_limit_bytes=4 * 1024 * 1024),
    )(grad_q, grad_k, grad_v, grad_w)
    return (grad_q[None], grad_k[None], grad_v[None], grad_w)


def solution(mesh):
    in_specs = (
        P("dp", "ctx", "head"),
        P("dp", "ctx", "head"),
        P("dp", "ctx", "head"),
        P("dp", "ctx", "head"),
        P("dp", ("ctx", "head"), None),
        P("dp", None),
        P(),
        P(),
    )
    out_specs = (
        P("dp", "ctx", "head"),
        P("dp", "ctx", "head"),
        P("dp", "ctx", "head"),
        P(("ctx", "dp"), None, "head"),
    )
    return jax.shard_map(local, mesh=mesh, in_specs=in_specs, out_specs=out_specs, check_vma=False)
```

```python
import math

import jax
import jax.numpy as jnp
from jax import lax
from jax.experimental import pallas as pl
from jax.experimental.pallas import tpu as pltpu
from jax.sharding import PartitionSpec as P

HD = 128
BLK = 128
NCTX = 16
NZ = 8
NY = 4
NH = 8
GROUP = 8
WIN = 1280
ROWS = 160
BACK = 4
KEYS = (BACK + 1) * BLK
NEG = -1e30
TERMS = 4
PARTS = ((0, 2), (2, 4))
SCALE = 1.0 / math.sqrt(HD)
MESH = pl.DeviceIdType.MESH


def dot(a, b, dims):
    return lax.dot_general(a, b, (dims, ((), ())), preferred_element_type=jnp.float32)


def kernel(
    q_hbm, k_hbm, v_hbm, g_hbm, x_hbm, doc_ref, rank_ref, take_ref,
    oq_ref, ok_ref, ov_ref, ow_ref,
    qbuf, gbuf, xbuf, kall, vall, bias, probs, pushes, dsb, pbb, vsend, vrecv, ksend, krecv,
    xall, xt, gv, gk, acc_v, acc_k, e1, u2, e2,
    loc_sem, a_send, a_recv, x1_send, x1_recv, x2_send, x2_recv,
    c_send, c_recv, d_send, d_recv, e_send, e_recv,
):
    c = lax.axis_index("ctx")
    h = lax.axis_index("head")
    d = lax.axis_index("dp")
    z, xl = c // 2, c % 2
    xh, y = h // NY, h % NY
    side = z % 2
    way = 1 - 2 * side

    def ctx(delta):
        return {"ctx": (c + delta + NCTX) % NCTX}

    def head_index(dx, dy):
        return ((xh + dx) % 2) * NY + (y + dy + NY) % NY

    def head(dx, dy):
        return {"head": head_index(dx, dy)}

    core_peer = {"dp": 1 - d}
    side_peer = {"ctx": c + 2 * way}
    x_peer = {"ctx": c + 1 - 2 * xl}
    far_peer = {"ctx": c + 2 * way + 1 - 2 * xl}
    reach = {1: -way, 2: 2 * way, 3: -3 * way}

    barrier = pltpu.get_barrier_semaphore()
    peers = [ctx(s) for s in (1, 2, 3, 4, -1, -2, -3, -4)] + [ctx(-6 * way)]
    peers += [head(1, 0), head(0, 1), head(0, 2), head(0, 3), core_peer]
    for peer in peers:
        pl.semaphore_signal(barrier, inc=1, device_id=peer, device_id_type=MESH)

    local = []

    def fetch(src, dst):
        copy = pltpu.make_async_copy(src, dst, loc_sem.at[len(local)])
        copy.start()
        local.append(copy)

    fetch(k_hbm, kall.at[pl.ds(0, BLK)])
    fetch(v_hbm, vall.at[pl.ds(0, BLK)])
    fetch(x_hbm, xbuf)
    for n in range(GROUP):
        fetch(q_hbm.at[:, pl.ds(n * HD, HD)], qbuf.at[pl.ds(n * BLK, BLK)])
        fetch(g_hbm.at[:, pl.ds(n * HD, HD)], gbuf.at[pl.ds(n * BLK, BLK)])

    down = lax.broadcasted_iota(jnp.int32, (BLK, BLK), 0)
    across = lax.broadcasted_iota(jnp.int32, (BLK, BLK), 1)
    excluded = jnp.int32(0)
    end = jnp.int32(0)
    count_down = jnp.zeros((BLK, BLK), jnp.int32)
    count_across = jnp.zeros((BLK, BLK), jnp.int32)
    for b in range(NCTX):
        excluded = excluded + jnp.where(rank_ref[b] < 0, b, 0)
        end = end + take_ref[b]
        count_down = count_down + jnp.where(down >= end, 1, 0)
        count_across = count_across + jnp.where(across >= end, 1, 0)
    taken_down = count_down - jnp.where(count_down > excluded, 1, 0)
    taken_across = count_across - jnp.where(count_across > excluded, 1, 0)
    my_rank = jnp.full((BLK, BLK), rank_ref[c], jnp.int32)
    slot_t = jnp.where(my_rank < 0, taken_across, my_rank)
    doc_t = jnp.broadcast_to(
        doc_ref[:, pl.ds(pl.multiple_of(c * BLK, BLK), BLK)], (BLK, BLK)
    )
    for j in range(BACK + 1):
        b = (c - j + NCTX) % NCTX
        rank = jnp.full((BLK, BLK), rank_ref[b], jnp.int32)
        gap = slot_t - jnp.where(rank < 0, taken_down, rank)
        doc_u = jnp.broadcast_to(
            doc_ref[:, pl.ds(pl.multiple_of(b * BLK, BLK), BLK)], (BLK, BLK)
        ).T
        order = (c * BLK + across) - (b * BLK + down)
        seen = (doc_u == doc_t) & (order >= 0) & (gap >= 0) & (gap <= 2)
        bias[pl.ds(j * BLK, BLK), :] = jnp.where(seen, 0.0, NEG)

    for copy in local:
        copy.wait()
    xall[0, h] = xbuf[:, pl.ds(pl.multiple_of((z // 2) * WIN, 128), WIN)]

    chunks = [pl.ds(p * 2 * BLK, 2 * BLK) for p in range(GROUP // 2)]
    tops = [jnp.full((1, 2 * BLK), NEG, jnp.float32) for _ in chunks]

    def score(first, last):
        rows = pl.ds(first * BLK, (last - first) * BLK)
        hidden = bias[rows, :]
        hidden = jnp.concatenate([hidden, hidden], 1)
        for p, cols in enumerate(chunks):
            part = dot(kall[rows, :], qbuf[cols, :], ((1,), (1,))) * SCALE + hidden
            probs[rows, cols] = part
            tops[p] = jnp.maximum(tops[p], jnp.max(part, 0, keepdims=True))

    def value_products(first, last):
        rows = pl.ds(first * BLK, (last - first) * BLK)
        for cols in chunks:
            pushes[rows, cols] = dot(vall[rows, :], gbuf[cols, :], ((1,), (1,)))

    score(0, 1)
    value_products(0, 1)
    pl.semaphore_wait(barrier, len(peers))

    def push(src, dst, send, recv, peer):
        copy = pltpu.make_async_remote_copy(
            src_ref=src, dst_ref=dst, send_sem=send, recv_sem=recv,
            device_id=peer, device_id_type=MESH,
        )
        copy.start()
        return copy

    a_copies = {}

    def hand_on(kind, held, j, source, peer):
        a_copies[kind, j] = push(
            held.at[pl.ds(source, BLK)], held.at[pl.ds(j * BLK, BLK)],
            a_send.at[kind, j - 1], a_recv.at[kind, j - 1], peer,
        )

    hand_on(0, kall, 4, 0, ctx(4))
    hand_on(1, vall, 4, 0, ctx(4))
    hand_on(0, kall, 2, 0, ctx(2))
    hand_on(0, kall, 1, 0, ctx(1))
    x1_copies = []
    for r in (3, 2, 1):
        there = (z + reach[r] + NZ) % NZ // 2
        copy = push(
            xbuf.at[:, pl.ds(pl.multiple_of(there * WIN, 128), WIN)],
            xall.at[r, h], x1_send.at[r - 1], x1_recv.at[r - 1], ctx(2 * reach[r]),
        )
        x1_copies.append((r, copy))
    hand_on(1, vall, 2, 0, ctx(2))
    hand_on(1, vall, 1, 0, ctx(1))
    third = pl.multiple_of(xl * BACK * BLK, BLK)
    third_peer = {"ctx": (c + 3 - 4 * xl + NCTX) % NCTX}
    for kind, held in ((0, kall), (1, vall)):
        a_copies[kind, 4].wait_recv()
        hand_on(kind, held, 3, third, third_peer)
    score(4, 5)
    value_products(4, 5)
    x2_copies = {}

    def spread(step, group, at, peer):
        first, last = PARTS[group]
        part = xall.at[pl.ds(first, last - first), at]
        x2_copies[step, group] = push(
            part, part, x2_send.at[group, step], x2_recv.at[group, step], peer
        )

    def spread_own(group):
        for copy in x1_copies:
            if PARTS[group][0] <= copy[0] < PARTS[group][1]:
                copy[1].wait_recv()
        spread(0, group, h, head(1, 0))
        spread(1, group, h, head(0, 1))
        spread(2, group, h, head(0, -1))

    def spread_own_on(group):
        x2_copies[1, group].wait_recv()
        spread(3, group, head_index(0, -1), head(0, 1))

    def spread_other(group):
        x2_copies[0, group].wait_recv()
        spread(4, group, head_index(1, 0), head(0, 1))
        spread(5, group, head_index(1, 0), head(0, -1))

    def spread_other_on(group):
        x2_copies[5, group].wait_recv()
        spread(6, group, head_index(1, 1), head(0, -1))

    spread_own(0)
    spread_own(1)
    for j in (1, 2):
        a_copies[0, j].wait_recv()
    score(1, 3)
    a_copies[0, 3].wait_recv()
    score(3, 4)

    inverse = []
    for p, cols in enumerate(chunks):
        weights = jnp.exp(probs[:, cols] - tops[p])
        probs[:, cols] = weights
        inverse.append(1.0 / jnp.sum(weights, 0, keepdims=True))
    inverse = jnp.concatenate(inverse, 1)
    c_copies = []

    def send_back(kind, j, held, received, grad):
        held[j - 1] = grad.astype(jnp.bfloat16)
        c_copies.append(
            push(
                held.at[j - 1], received.at[j - 1],
                c_send.at[kind, j - 1], c_recv.at[kind, j - 1], ctx(-j),
            )
        )

    for j in (1, 3, 2, 4, 0):
        rows = pl.ds(j * BLK, BLK)
        share = probs[rows, :] * inverse
        probs[rows, :] = share
        pbb[rows, :] = share.astype(jnp.bfloat16)
        own_v = dot(pbb[rows, :], gbuf[...], ((1,), (0,)))
        if j > 0:
            send_back(0, j, vsend, vrecv, own_v)

    spread_own_on(0)

    for j in (1, 2):
        a_copies[1, j].wait_recv()
    value_products(1, 3)
    a_copies[1, 3].wait_recv()
    value_products(3, 4)
    delta = [
        jnp.sum(probs[:, cols] * pushes[:, cols], 0, keepdims=True) for cols in chunks
    ]
    delta = jnp.concatenate(delta, 1)
    for j in (1, 3, 2, 4, 0):
        rows = pl.ds(j * BLK, BLK)
        change = probs[rows, :] * (pushes[rows, :] - delta)
        dsb[rows, :] = change.astype(jnp.bfloat16)
        own_k = dot(dsb[rows, :], qbuf[...], ((1,), (0,))) * SCALE
        if j > 0:
            send_back(1, j, ksend, krecv, own_k)

    spread_other(0)
    spread_other(1)
    spread_own_on(1)

    d_copies = {}

    def collect(kind, own, received, copies, held, out_ref):
        for copy in copies:
            copy.wait_recv()
        for j in range(BACK):
            own = own + received[j].astype(jnp.float32)
        final = own.astype(jnp.bfloat16)
        held[0] = final
        out_ref[...] = final
        for r in (3, 2, 1):
            d_copies[kind, r] = push(
                held.at[0], held.at[r],
                d_send.at[kind, r - 1], d_recv.at[kind, r - 1], ctx(2 * reach[r]),
            )

    collect(0, own_v, vrecv, c_copies[:BACK], gv, ov_ref)

    def query_grads(p, carry):
        cols = pl.ds(pl.multiple_of(p * 2 * BLK, 2 * BLK), 2 * BLK)
        both = dot(dsb[:, cols], kall[...], ((0,), (0,))) * SCALE
        both = both.astype(jnp.bfloat16)
        oq_ref[:, cols] = jnp.concatenate([both[:BLK], both[BLK:]], 1)
        return carry

    lax.fori_loop(0, GROUP // 2, query_grads, 0)

    spread_other_on(0)
    spread_other_on(1)

    collect(1, own_k, krecv, c_copies[BACK:], gk, ok_ref)

    def flip(group):
        for step in (2, 3, 4, 6):
            x2_copies[step, group].wait_recv()
        for r in range(*PARTS[group]):
            xt[:, pl.ds(r * BLK, BLK)] = xall[r].reshape(BLK, WIN).T

    e_copies = {}

    def product(kind, held, acc, at_side, first, last):
        for r in range(max(first, 1), last):
            if (kind, r) not in landed:
                landed.add((kind, r))
                d_copies[kind, r].wait_recv()
        rows = pl.ds(pl.multiple_of(at_side * (WIN // 2), 128), WIN // 2)
        terms = held[first:last].reshape((last - first) * BLK, HD)
        part = dot(xt[rows, first * BLK : last * BLK], terms, ((1,), (0,)))
        part = part.reshape(2, 2, ROWS, HD)
        acc[at_side] = part if first == 0 else acc[at_side] + part

    landed = set()

    def exchange(kind, i, src, dst, peer):
        e_copies[kind, i] = push(src, dst, e_send.at[kind, i], e_recv.at[kind, i], peer)

    def send_core(kind, acc, i, at_side):
        exchange(kind, i, acc.at[at_side, :, 1 - d], e1.at[kind, at_side], core_peer)

    def send_other(kind, acc, i, at_side, at_x, peer):
        both = acc[at_side, at_x, d] + e1[kind, at_side, at_x]
        u2[kind, i] = both.astype(jnp.bfloat16)
        exchange(kind, i + 2, u2.at[kind, i], e2.at[kind, i], peer)

    def send_others(kind, acc):
        e_copies[kind, 0].wait_recv()
        send_other(kind, acc, 0, 1 - side, 1 - xl, far_peer)
        send_other(kind, acc, 1, 1 - side, xl, side_peer)
        e_copies[kind, 1].wait_recv()
        send_other(kind, acc, 2, side, 1 - xl, x_peer)

    def total(kind, acc):
        whole = acc[side, xl, d] + e1[kind, side, xl]
        for i in range(3):
            e_copies[kind, i + 2].wait_recv()
            whole = whole + e2[kind, i].astype(jnp.float32)
        return whole

    flip(0)
    for at_side in (1 - side, side):
        product(0, gv, acc_v, at_side, 0, 2)
    flip(1)
    for i, at_side in enumerate((1 - side, side)):
        product(0, gv, acc_v, at_side, 2, TERMS)
        send_core(0, acc_v, i, at_side)
    for at_side in (1 - side, side):
        product(1, gk, acc_k, at_side, 0, TERMS - 1)
    send_others(0, acc_v)
    for i, at_side in enumerate((1 - side, side)):
        product(1, gk, acc_k, at_side, TERMS - 1, TERMS)
        send_core(1, acc_k, i, at_side)
    send_others(1, acc_k)
    ow_ref[1] = total(0, acc_v)
    ow_ref[0] = total(1, acc_k)

    for copy in list(a_copies.values()) + list(d_copies.values()) + c_copies + list(e_copies.values()):
        copy.wait_send()
    for copy in [copy for _, copy in x1_copies] + list(x2_copies.values()):
        copy.wait_send()


def finish(q_ref, k_ref, v_ref, w_ref, oq_ref, ok_ref, ov_ref, ow_ref):
    oq_ref[...] = q_ref[...]
    ok_ref[...] = k_ref[...]
    ov_ref[...] = v_ref[...]
    ow_ref[:, 0, :] = w_ref[0]
    ow_ref[:, 1, :] = w_ref[1]


def local(queries, keys, values, grad_out, layer_inputs, doc_ids, member_rank, take_count):
    bf16, f32 = jnp.bfloat16, jnp.float32
    hbm = pl.BlockSpec(memory_space=pltpu.HBM)
    vmem = pl.BlockSpec(memory_space=pltpu.VMEM)
    smem = pl.BlockSpec(memory_space=pltpu.SMEM)
    dma = pltpu.SemaphoreType.DMA
    grad_q, grad_k, grad_v, grad_w = pl.pallas_call(
        kernel,
        out_shape=[
            pltpu.VMEM((BLK, GROUP * HD), bf16),
            pltpu.VMEM((BLK, HD), bf16),
            pltpu.VMEM((BLK, HD), bf16),
            pltpu.VMEM((2, ROWS, HD), f32),
        ],
        in_specs=[hbm] * 5 + [vmem, smem, smem],
        out_specs=[vmem] * 4,
        scratch_shapes=[
            pltpu.VMEM((GROUP * BLK, HD), bf16),
            pltpu.VMEM((GROUP * BLK, HD), bf16),
            pltpu.VMEM((BLK // NH, TERMS * WIN), bf16),
            pltpu.VMEM((KEYS, HD), bf16),
            pltpu.VMEM((KEYS, HD), bf16),
            pltpu.VMEM((KEYS, BLK), f32),
            pltpu.VMEM((KEYS, GROUP * BLK), f32),
            pltpu.VMEM((KEYS, GROUP * BLK), f32),
            pltpu.VMEM((KEYS, GROUP * BLK), bf16),
            pltpu.VMEM((KEYS, GROUP * BLK), bf16),
            pltpu.VMEM((BACK, BLK, HD), bf16),
            pltpu.VMEM((BACK, BLK, HD), bf16),
            pltpu.VMEM((BACK, BLK, HD), bf16),
            pltpu.VMEM((BACK, BLK, HD), bf16),
            pltpu.VMEM((TERMS, NH, BLK // NH, WIN), bf16),
            pltpu.VMEM((WIN, TERMS * BLK), bf16),
            pltpu.VMEM((TERMS, BLK, HD), bf16),
            pltpu.VMEM((TERMS, BLK, HD), bf16),
            pltpu.VMEM((2, 2, 2, ROWS, HD), f32),
            pltpu.VMEM((2, 2, 2, ROWS, HD), f32),
            pltpu.VMEM((2, 2, 2, ROWS, HD), f32),
            pltpu.VMEM((2, 3, ROWS, HD), bf16),
            pltpu.VMEM((2, 3, ROWS, HD), bf16),
            dma((2 * GROUP + 3,)),
            dma((2, BACK)),
            dma((2, BACK)),
            dma((TERMS - 1,)),
            dma((TERMS - 1,)),
            dma((len(PARTS), 7)),
            dma((len(PARTS), 7)),
            dma((2, BACK)),
            dma((2, BACK)),
            dma((2, TERMS - 1)),
            dma((2, TERMS - 1)),
            dma((2, 5)),
            dma((2, 5)),
        ],
        compiler_params=pltpu.CompilerParams(
            collective_id=0, has_side_effects=True, vmem_limit_bytes=60 * 1024 * 1024
        ),
        cost_estimate=pl.CostEstimate(
            flops=1300000000, bytes_accessed=2000000, transcendentals=700000
        ),
    )(
        queries[0], keys[0], values[0], grad_out[0], layer_inputs[0],
        doc_ids, member_rank, take_count,
    )
    grad_q, grad_k, grad_v, grad_w = pl.pallas_call(
        finish,
        out_shape=[
            jax.ShapeDtypeStruct((BLK, GROUP * HD), bf16),
            jax.ShapeDtypeStruct((BLK, HD), bf16),
            jax.ShapeDtypeStruct((BLK, HD), bf16),
            jax.ShapeDtypeStruct((ROWS, 2, HD), f32),
        ],
        in_specs=[vmem] * 4,
        out_specs=[vmem] * 4,
        compiler_params=pltpu.CompilerParams(vmem_limit_bytes=4 * 1024 * 1024),
    )(grad_q, grad_k, grad_v, grad_w)
    return (grad_q[None], grad_k[None], grad_v[None], grad_w)


def solution(mesh):
    in_specs = (
        P("dp", "ctx", "head"),
        P("dp", "ctx", "head"),
        P("dp", "ctx", "head"),
        P("dp", "ctx", "head"),
        P("dp", ("ctx", "head"), None),
        P("dp", None),
        P(),
        P(),
    )
    out_specs = (
        P("dp", "ctx", "head"),
        P("dp", "ctx", "head"),
        P("dp", "ctx", "head"),
        P(("ctx", "dp"), None, "head"),
    )
    return jax.shard_map(local, mesh=mesh, in_specs=in_specs, out_specs=out_specs, check_vma=False)
```

```python
import math

import jax
import jax.numpy as jnp
from jax import lax
from jax.experimental import pallas as pl
from jax.experimental.pallas import tpu as pltpu
from jax.sharding import PartitionSpec as P

HD = 128
BLK = 128
NCTX = 16
NZ = 8
NY = 4
NH = 8
GROUP = 8
WIN = 1280
ROWS = 160
BACK = 4
KEYS = (BACK + 1) * BLK
NEG = -1e30
TERMS = 4
PARTS = ((0, 2), (2, 4))
SCALE = 1.0 / math.sqrt(HD)
MESH = pl.DeviceIdType.MESH


def dot(a, b, dims):
    return lax.dot_general(a, b, (dims, ((), ())), preferred_element_type=jnp.float32)


def kernel(
    q_hbm, k_hbm, v_hbm, g_hbm, x_hbm, doc_ref, rank_ref, take_ref,
    oq_ref, ok_ref, ov_ref, ow_ref,
    qbuf, gbuf, xbuf, kall, vall, bias, probs, pushes, dsb, pbb, vsend, vrecv, ksend, krecv,
    xall, xt, gv, gk, acc_v, acc_k, e1, u2, e2,
    loc_sem, a_send, a_recv, x1_send, x1_recv, x2_send, x2_recv,
    c_send, c_recv, d_send, d_recv, e_send, e_recv,
):
    c = lax.axis_index("ctx")
    h = lax.axis_index("head")
    d = lax.axis_index("dp")
    z, xl = c // 2, c % 2
    xh, y = h // NY, h % NY
    side = z % 2
    way = 1 - 2 * side

    def ctx(delta):
        return {"ctx": (c + delta + NCTX) % NCTX}

    def head_index(dx, dy):
        return ((xh + dx) % 2) * NY + (y + dy + NY) % NY

    def head(dx, dy):
        return {"head": head_index(dx, dy)}

    core_peer = {"dp": 1 - d}
    side_peer = {"ctx": c + 2 * way}
    x_peer = {"ctx": c + 1 - 2 * xl}
    far_peer = {"ctx": c + 2 * way + 1 - 2 * xl}
    reach = {1: -way, 2: 2 * way, 3: -3 * way}

    barrier = pltpu.get_barrier_semaphore()
    peers = [ctx(s) for s in (1, 2, 3, 4, -1, -2, -3, -4)] + [ctx(-6 * way)]
    peers += [head(1, 0), head(0, 1), head(0, 2), head(0, 3), core_peer]
    for peer in peers:
        pl.semaphore_signal(barrier, inc=1, device_id=peer, device_id_type=MESH)

    local = []

    def fetch(src, dst):
        copy = pltpu.make_async_copy(src, dst, loc_sem.at[len(local)])
        copy.start()
        local.append(copy)

    fetch(k_hbm, kall.at[pl.ds(0, BLK)])
    fetch(v_hbm, vall.at[pl.ds(0, BLK)])
    fetch(x_hbm, xbuf)
    for n in range(GROUP):
        fetch(q_hbm.at[:, pl.ds(n * HD, HD)], qbuf.at[pl.ds(n * BLK, BLK)])
        fetch(g_hbm.at[:, pl.ds(n * HD, HD)], gbuf.at[pl.ds(n * BLK, BLK)])

    down = lax.broadcasted_iota(jnp.int32, (BLK, BLK), 0)
    across = lax.broadcasted_iota(jnp.int32, (BLK, BLK), 1)
    excluded = jnp.int32(0)
    end = jnp.int32(0)
    count_down = jnp.zeros((BLK, BLK), jnp.int32)
    count_across = jnp.zeros((BLK, BLK), jnp.int32)
    for b in range(NCTX):
        excluded = excluded + jnp.where(rank_ref[b] < 0, b, 0)
        end = end + take_ref[b]
        count_down = count_down + jnp.where(down >= end, 1, 0)
        count_across = count_across + jnp.where(across >= end, 1, 0)
    taken_down = count_down - jnp.where(count_down > excluded, 1, 0)
    taken_across = count_across - jnp.where(count_across > excluded, 1, 0)
    my_rank = jnp.full((BLK, BLK), rank_ref[c], jnp.int32)
    slot_t = jnp.where(my_rank < 0, taken_across, my_rank)
    doc_t = jnp.broadcast_to(
        doc_ref[:, pl.ds(pl.multiple_of(c * BLK, BLK), BLK)], (BLK, BLK)
    )
    for j in range(BACK + 1):
        b = (c - j + NCTX) % NCTX
        rank = jnp.full((BLK, BLK), rank_ref[b], jnp.int32)
        gap = slot_t - jnp.where(rank < 0, taken_down, rank)
        doc_u = jnp.broadcast_to(
            doc_ref[:, pl.ds(pl.multiple_of(b * BLK, BLK), BLK)], (BLK, BLK)
        ).T
        order = (c * BLK + across) - (b * BLK + down)
        seen = (doc_u == doc_t) & (order >= 0) & (gap >= 0) & (gap <= 2)
        bias[pl.ds(j * BLK, BLK), :] = jnp.where(seen, 0.0, NEG)

    for copy in local:
        copy.wait()
    xall[0, h] = xbuf[:, pl.ds(pl.multiple_of((z // 2) * WIN, 128), WIN)]

    chunks = [pl.ds(p * 2 * BLK, 2 * BLK) for p in range(GROUP // 2)]
    tops = [jnp.full((1, 2 * BLK), NEG, jnp.float32) for _ in chunks]

    def score(first, last):
        rows = pl.ds(first * BLK, (last - first) * BLK)
        hidden = bias[rows, :]
        hidden = jnp.concatenate([hidden, hidden], 1)
        for p, cols in enumerate(chunks):
            part = dot(kall[rows, :], qbuf[cols, :], ((1,), (1,))) * SCALE + hidden
            probs[rows, cols] = part
            tops[p] = jnp.maximum(tops[p], jnp.max(part, 0, keepdims=True))

    def value_products(first, last):
        rows = pl.ds(first * BLK, (last - first) * BLK)
        for cols in chunks:
            pushes[rows, cols] = dot(vall[rows, :], gbuf[cols, :], ((1,), (1,)))

    score(0, 1)
    value_products(0, 1)
    pl.semaphore_wait(barrier, len(peers))

    def push(src, dst, send, recv, peer):
        copy = pltpu.make_async_remote_copy(
            src_ref=src, dst_ref=dst, send_sem=send, recv_sem=recv,
            device_id=peer, device_id_type=MESH,
        )
        copy.start()
        return copy

    a_copies = {}

    def hand_on(kind, held, j, source, peer):
        a_copies[kind, j] = push(
            held.at[pl.ds(source, BLK)], held.at[pl.ds(j * BLK, BLK)],
            a_send.at[kind, j - 1], a_recv.at[kind, j - 1], peer,
        )

    hand_on(0, kall, 4, 0, ctx(4))
    hand_on(1, vall, 4, 0, ctx(4))
    hand_on(0, kall, 2, 0, ctx(2))
    hand_on(0, kall, 1, 0, ctx(1))
    x1_copies = []
    for r in (3, 2, 1):
        there = (z + reach[r] + NZ) % NZ // 2
        copy = push(
            xbuf.at[:, pl.ds(pl.multiple_of(there * WIN, 128), WIN)],
            xall.at[r, h], x1_send.at[r - 1], x1_recv.at[r - 1], ctx(2 * reach[r]),
        )
        x1_copies.append((r, copy))
    hand_on(1, vall, 2, 0, ctx(2))
    hand_on(1, vall, 1, 0, ctx(1))
    third = pl.multiple_of(xl * BACK * BLK, BLK)
    third_peer = {"ctx": (c + 3 - 4 * xl + NCTX) % NCTX}
    for kind, held in ((0, kall), (1, vall)):
        a_copies[kind, 4].wait_recv()
        hand_on(kind, held, 3, third, third_peer)
    score(4, 5)
    value_products(4, 5)
    x2_copies = {}

    def spread(step, group, at, peer):
        first, last = PARTS[group]
        part = xall.at[pl.ds(first, last - first), at]
        x2_copies[step, group] = push(
            part, part, x2_send.at[group, step], x2_recv.at[group, step], peer
        )

    def spread_own(group):
        for copy in x1_copies:
            if PARTS[group][0] <= copy[0] < PARTS[group][1]:
                copy[1].wait_recv()
        spread(1, group, h, head(0, 1))
        spread(2, group, h, head(0, -1))
        spread(0, group, h, head(1, 0))

    def spread_own_on(group):
        x2_copies[1, group].wait_recv()
        spread(3, group, head_index(0, -1), head(0, 1))

    def spread_other(group):
        x2_copies[0, group].wait_recv()
        spread(4, group, head_index(1, 0), head(0, 1))
        spread(5, group, head_index(1, 0), head(0, -1))

    def spread_other_on(group):
        x2_copies[5, group].wait_recv()
        spread(6, group, head_index(1, 1), head(0, -1))

    spread_own(0)
    spread_own(1)
    for j in (1, 2):
        a_copies[0, j].wait_recv()
    score(1, 3)
    a_copies[0, 3].wait_recv()
    score(3, 4)

    inverse = []
    for p, cols in enumerate(chunks):
        weights = jnp.exp(probs[:, cols] - tops[p])
        probs[:, cols] = weights
        inverse.append(1.0 / jnp.sum(weights, 0, keepdims=True))
    inverse = jnp.concatenate(inverse, 1)
    c_copies = []

    def send_back(kind, j, held, received, grad):
        held[j - 1] = grad.astype(jnp.bfloat16)
        c_copies.append(
            push(
                held.at[j - 1], received.at[j - 1],
                c_send.at[kind, j - 1], c_recv.at[kind, j - 1], ctx(-j),
            )
        )

    for j in (1, 3, 2, 4, 0):
        rows = pl.ds(j * BLK, BLK)
        share = probs[rows, :] * inverse
        probs[rows, :] = share
        pbb[rows, :] = share.astype(jnp.bfloat16)
        own_v = dot(pbb[rows, :], gbuf[...], ((1,), (0,)))
        if j > 0:
            send_back(0, j, vsend, vrecv, own_v)

    spread_own_on(0)

    for j in (1, 2):
        a_copies[1, j].wait_recv()
    value_products(1, 3)
    a_copies[1, 3].wait_recv()
    value_products(3, 4)
    delta = [
        jnp.sum(probs[:, cols] * pushes[:, cols], 0, keepdims=True) for cols in chunks
    ]
    delta = jnp.concatenate(delta, 1)
    for j in (1, 3, 2, 4, 0):
        rows = pl.ds(j * BLK, BLK)
        change = probs[rows, :] * (pushes[rows, :] - delta)
        dsb[rows, :] = change.astype(jnp.bfloat16)
        own_k = dot(dsb[rows, :], qbuf[...], ((1,), (0,))) * SCALE
        if j > 0:
            send_back(1, j, ksend, krecv, own_k)

    spread_other(0)
    spread_other(1)
    spread_own_on(1)

    d_copies = {}

    def collect(kind, own, received, copies, held, out_ref):
        for copy in copies:
            copy.wait_recv()
        for j in range(BACK):
            own = own + received[j].astype(jnp.float32)
        final = own.astype(jnp.bfloat16)
        held[0] = final
        out_ref[...] = final
        for r in (3, 2, 1):
            d_copies[kind, r] = push(
                held.at[0], held.at[r],
                d_send.at[kind, r - 1], d_recv.at[kind, r - 1], ctx(2 * reach[r]),
            )

    collect(0, own_v, vrecv, c_copies[:BACK], gv, ov_ref)

    def query_grads(p, carry):
        cols = pl.ds(pl.multiple_of(p * 2 * BLK, 2 * BLK), 2 * BLK)
        both = dot(dsb[:, cols], kall[...], ((0,), (0,))) * SCALE
        both = both.astype(jnp.bfloat16)
        oq_ref[:, cols] = jnp.concatenate([both[:BLK], both[BLK:]], 1)
        return carry

    lax.fori_loop(0, GROUP // 2, query_grads, 0)

    spread_other_on(0)
    spread_other_on(1)

    collect(1, own_k, krecv, c_copies[BACK:], gk, ok_ref)

    def flip(group):
        for step in (2, 3, 4, 6):
            x2_copies[step, group].wait_recv()
        for r in range(*PARTS[group]):
            xt[:, pl.ds(r * BLK, BLK)] = xall[r].reshape(BLK, WIN).T

    e_copies = {}

    def product(kind, held, acc, at_side, first, last):
        for r in range(max(first, 1), last):
            if (kind, r) not in landed:
                landed.add((kind, r))
                d_copies[kind, r].wait_recv()
        rows = pl.ds(pl.multiple_of(at_side * (WIN // 2), 128), WIN // 2)
        terms = held[first:last].reshape((last - first) * BLK, HD)
        part = dot(xt[rows, first * BLK : last * BLK], terms, ((1,), (0,)))
        part = part.reshape(2, 2, ROWS, HD)
        acc[at_side] = part if first == 0 else acc[at_side] + part

    landed = set()

    def exchange(kind, i, src, dst, peer):
        e_copies[kind, i] = push(src, dst, e_send.at[kind, i], e_recv.at[kind, i], peer)

    def send_core(kind, acc, i, at_side):
        exchange(kind, i, acc.at[at_side, :, 1 - d], e1.at[kind, at_side], core_peer)

    def send_other(kind, acc, i, at_side, at_x, peer):
        both = acc[at_side, at_x, d] + e1[kind, at_side, at_x]
        u2[kind, i] = both.astype(jnp.bfloat16)
        exchange(kind, i + 2, u2.at[kind, i], e2.at[kind, i], peer)

    def send_others(kind, acc):
        e_copies[kind, 0].wait_recv()
        send_other(kind, acc, 0, 1 - side, 1 - xl, far_peer)
        send_other(kind, acc, 1, 1 - side, xl, side_peer)
        e_copies[kind, 1].wait_recv()
        send_other(kind, acc, 2, side, 1 - xl, x_peer)

    def total(kind, acc):
        whole = acc[side, xl, d] + e1[kind, side, xl]
        for i in range(3):
            e_copies[kind, i + 2].wait_recv()
            whole = whole + e2[kind, i].astype(jnp.float32)
        return whole

    flip(0)
    for at_side in (1 - side, side):
        product(0, gv, acc_v, at_side, 0, 2)
    flip(1)
    for i, at_side in enumerate((1 - side, side)):
        product(0, gv, acc_v, at_side, 2, TERMS)
        send_core(0, acc_v, i, at_side)
    for at_side in (1 - side, side):
        product(1, gk, acc_k, at_side, 0, TERMS - 1)
    send_others(0, acc_v)
    for i, at_side in enumerate((1 - side, side)):
        product(1, gk, acc_k, at_side, TERMS - 1, TERMS)
        send_core(1, acc_k, i, at_side)
    send_others(1, acc_k)
    ow_ref[1] = total(0, acc_v)
    ow_ref[0] = total(1, acc_k)

    for copy in list(a_copies.values()) + list(d_copies.values()) + c_copies + list(e_copies.values()):
        copy.wait_send()
    for copy in [copy for _, copy in x1_copies] + list(x2_copies.values()):
        copy.wait_send()


def finish(q_ref, k_ref, v_ref, w_ref, oq_ref, ok_ref, ov_ref, ow_ref):
    oq_ref[...] = q_ref[...]
    ok_ref[...] = k_ref[...]
    ov_ref[...] = v_ref[...]
    ow_ref[:, 0, :] = w_ref[0]
    ow_ref[:, 1, :] = w_ref[1]


def local(queries, keys, values, grad_out, layer_inputs, doc_ids, member_rank, take_count):
    bf16, f32 = jnp.bfloat16, jnp.float32
    hbm = pl.BlockSpec(memory_space=pltpu.HBM)
    vmem = pl.BlockSpec(memory_space=pltpu.VMEM)
    smem = pl.BlockSpec(memory_space=pltpu.SMEM)
    dma = pltpu.SemaphoreType.DMA
    grad_q, grad_k, grad_v, grad_w = pl.pallas_call(
        kernel,
        out_shape=[
            pltpu.VMEM((BLK, GROUP * HD), bf16),
            pltpu.VMEM((BLK, HD), bf16),
            pltpu.VMEM((BLK, HD), bf16),
            pltpu.VMEM((2, ROWS, HD), f32),
        ],
        in_specs=[hbm] * 5 + [vmem, smem, smem],
        out_specs=[vmem] * 4,
        scratch_shapes=[
            pltpu.VMEM((GROUP * BLK, HD), bf16),
            pltpu.VMEM((GROUP * BLK, HD), bf16),
            pltpu.VMEM((BLK // NH, TERMS * WIN), bf16),
            pltpu.VMEM((KEYS, HD), bf16),
            pltpu.VMEM((KEYS, HD), bf16),
            pltpu.VMEM((KEYS, BLK), f32),
            pltpu.VMEM((KEYS, GROUP * BLK), f32),
            pltpu.VMEM((KEYS, GROUP * BLK), f32),
            pltpu.VMEM((KEYS, GROUP * BLK), bf16),
            pltpu.VMEM((KEYS, GROUP * BLK), bf16),
            pltpu.VMEM((BACK, BLK, HD), bf16),
            pltpu.VMEM((BACK, BLK, HD), bf16),
            pltpu.VMEM((BACK, BLK, HD), bf16),
            pltpu.VMEM((BACK, BLK, HD), bf16),
            pltpu.VMEM((TERMS, NH, BLK // NH, WIN), bf16),
            pltpu.VMEM((WIN, TERMS * BLK), bf16),
            pltpu.VMEM((TERMS, BLK, HD), bf16),
            pltpu.VMEM((TERMS, BLK, HD), bf16),
            pltpu.VMEM((2, 2, 2, ROWS, HD), f32),
            pltpu.VMEM((2, 2, 2, ROWS, HD), f32),
            pltpu.VMEM((2, 2, 2, ROWS, HD), f32),
            pltpu.VMEM((2, 3, ROWS, HD), bf16),
            pltpu.VMEM((2, 3, ROWS, HD), bf16),
            dma((2 * GROUP + 3,)),
            dma((2, BACK)),
            dma((2, BACK)),
            dma((TERMS - 1,)),
            dma((TERMS - 1,)),
            dma((len(PARTS), 7)),
            dma((len(PARTS), 7)),
            dma((2, BACK)),
            dma((2, BACK)),
            dma((2, TERMS - 1)),
            dma((2, TERMS - 1)),
            dma((2, 5)),
            dma((2, 5)),
        ],
        compiler_params=pltpu.CompilerParams(
            collective_id=0, has_side_effects=True, vmem_limit_bytes=60 * 1024 * 1024
        ),
        cost_estimate=pl.CostEstimate(
            flops=1300000000, bytes_accessed=2000000, transcendentals=700000
        ),
    )(
        queries[0], keys[0], values[0], grad_out[0], layer_inputs[0],
        doc_ids, member_rank, take_count,
    )
    grad_q, grad_k, grad_v, grad_w = pl.pallas_call(
        finish,
        out_shape=[
            jax.ShapeDtypeStruct((BLK, GROUP * HD), bf16),
            jax.ShapeDtypeStruct((BLK, HD), bf16),
            jax.ShapeDtypeStruct((BLK, HD), bf16),
            jax.ShapeDtypeStruct((ROWS, 2, HD), f32),
        ],
        in_specs=[vmem] * 4,
        out_specs=[vmem] * 4,
        compiler_params=pltpu.CompilerParams(vmem_limit_bytes=4 * 1024 * 1024),
    )(grad_q, grad_k, grad_v, grad_w)
    return (grad_q[None], grad_k[None], grad_v[None], grad_w)


def solution(mesh):
    in_specs = (
        P("dp", "ctx", "head"),
        P("dp", "ctx", "head"),
        P("dp", "ctx", "head"),
        P("dp", "ctx", "head"),
        P("dp", ("ctx", "head"), None),
        P("dp", None),
        P(),
        P(),
    )
    out_specs = (
        P("dp", "ctx", "head"),
        P("dp", "ctx", "head"),
        P("dp", "ctx", "head"),
        P(("ctx", "dp"), None, "head"),
    )
    return jax.shard_map(local, mesh=mesh, in_specs=in_specs, out_specs=out_specs, check_vma=False)
```
